256 devices in a mesh: dp: 32 (over y, x, core), mp: 8 (over z).
Axes of the slice: x: 4, y: 4, z: 8, core: 2. Of those that a mesh axis runs over, the one named last changes fastest.
Arguments:
- patches: bfloat16 [4096, 588], P('dp'), may hold values from -6 to 6
- embed_weight: bfloat16 [6144, 588], P(('mp', 'dp')), may hold values from -0.25 to 0.25
- project_weight: bfloat16 [6144, 3, 3072], P('dp', None, 'mp'), may hold values from -0.078125 to 0.078125
- patch_counts: int32 [256], P('dp'), may hold values from 0 to 64, as said below
- segment_ids: int32 [4096], P('dp'), may hold values from -1 to 255, as said below
- targets: bfloat16 [4096, 3072], P('dp', 'mp'), may hold values from -4 to 4
Outputs:
- project_grad: float32 [6144, 3, 3072], P('dp', None, 'mp')
- loss_value: float32 [], replicated
The draws below stay inside these ranges and needn't reach their ends.
Inputs may be any that keep to these rules, and one draw needn't show every extreme that they name: `patch_counts`: entry 8 * i + j is the number of patches of image slot j of device i along dp, a multiple of 16, 0 for an empty slot; the counts of one device add up to at most 128, and some device reaches it. `segment_ids`: the rows of device i along dp hold its images whole, slot after slot, each row carrying the id 8 * i + slot of its image, then -1 on the rows left. A device in the upper half of dp holds more rows than the device half the axis away. On each device the images that end after its row 96 cover at most 64 rows. Those rows plus all the rows of the device half the axis away come to at most 96. Both bounds are reached.
All inputs are finite; a program needn't handle non-finite values.
Results may differ from the reference program's by a relative error of at most 0.012.
The reference program's roundings to bfloat16 on the way (of `embedded`, `normed`, `weights`, `out_grad`, `value_grad` and `score_grad`) count: a program that leaves them out, or rounds other values in their place, can miss the bound.
Values may be sent and summed in bfloat16 or wider, within the bound.
No kernel may reach another device: no remote copies, remote signals or barrier semaphores. Data moves between devices by JAX's collectives and lax.ppermute only.
A program may use at most 64 MiB of HBM per device.

```python
import math
import jax
import jax.numpy as jnp
from jax import lax

D = 6144
HEADS = 24
HD = 128
P_SIZE = 588
UNIT = 16
IMGS = 8
CAP = 128
ROWS = 4096
N_DP = 32


def split_units(totals, upper_draws):
    remain = totals
    portions = []
    for column in range(3):
        portion = jnp.minimum(remain, upper_draws[:, column])
        portions.append(portion)
        remain = remain - portion
    portions.append(remain)
    return jnp.stack(portions, axis=1)


def image_layout(key):
    pair_count = N_DP // 2
    base_key = jax.random.fold_in(key, 4242)
    tail_key, head_key, light_key, head_split, tail_split, light_split = jax.random.split(base_key, 6)
    tail_units = jax.random.randint(tail_key, (pair_count,), 2, 5)
    head_units = jnp.minimum(jax.random.randint(head_key, (pair_count,), 4, 6), 8 - tail_units)
    light_units = jax.random.randint(light_key, (pair_count,), 0, 7 - tail_units)
    head_units = head_units.at[0].set(5).at[1].set(4)
    tail_units = tail_units.at[0].set(3).at[1].set(4)
    light_units = light_units.at[0].set(3).at[1].set(2)
    head_parts = split_units(head_units, jax.random.randint(head_split, (pair_count, 4), 1, 5))
    tail_draws = jax.random.randint(tail_split, (pair_count, 4), 1, 5).at[1, 0].set(4)
    tail_parts = split_units(tail_units, tail_draws)
    light_parts = split_units(light_units, jax.random.randint(light_split, (pair_count, 4), 1, 5))
    heavy_side = jnp.concatenate([head_parts, tail_parts], axis=1)
    lighter = jnp.concatenate([light_parts, jnp.zeros_like(light_parts)], axis=1)
    unit_table = jnp.concatenate([lighter, heavy_side], axis=0)
    counts = (unit_table * UNIT).astype(jnp.int32)
    cumulative = jnp.cumsum(counts, axis=1)
    row_load = cumulative[:, -1]
    row_index = jnp.arange(CAP, dtype=jnp.int32)
    slot_index = jnp.sum((cumulative[:, None, :] <= row_index[None, :, None]).astype(jnp.int32), axis=-1)
    device = jnp.arange(N_DP, dtype=jnp.int32)[:, None]
    segment = jnp.where(row_index[None, :] < row_load[:, None], device * IMGS + slot_index, -1)
    return (counts.reshape(-1), segment.reshape(-1).astype(jnp.int32))


def draw_patch_counts(key, part):
    return image_layout(key)[0]


def draw_segment_ids(key, part):
    return image_layout(key)[1]


def level_of(stream_key, shape, pieces, smallest, high):
    level = 1.0
    for dim, shards_of in pieces:
        steps = jax.random.uniform(jax.random.fold_in(jax.random.fold_in(stream_key, 6), dim), (shards_of,), jnp.float32, smallest / len(pieces), high / len(pieces))
        level = level * jnp.repeat(jnp.exp(steps), shape[dim] // shards_of).reshape((-1,) + (1,) * (len(shape) - 1 - dim))
    return level


def normal_values(rng, extent, scale, limit, pieces=(), kind=jnp.bfloat16):
    loudness = level_of(rng, extent, pieces, -0.22, 0.18) if pieces else 1.0
    array = jax.random.normal(rng, extent, jnp.float32) * scale * loudness
    return jnp.minimum(jnp.maximum(array, -limit), limit).astype(kind)


def setup_inputs(seed: int = 0) -> dict:
    key_of = jax.random.split(jax.random.key(seed), 7)
    patches = normal_values(key_of[0], (ROWS, P_SIZE), 1.0, 6.0, ((0, 32),))
    embed_weight = normal_values(key_of[1], (D, P_SIZE), P_SIZE ** -0.5, 0.25, ((0, 256),))
    project_weight = normal_values(key_of[2], (D, 3, HEADS * HD), D ** -0.5, 0.078125, ((0, 32), (2, 8)))
    patch_counts = draw_patch_counts(jax.random.fold_in(key_of[6], 71), 0)
    segment_ids = draw_segment_ids(jax.random.fold_in(key_of[6], 71), 0)
    targets = normal_values(key_of[5], (ROWS, HEADS * HD), 0.5, 4.0, ((0, 32), (1, 8)))
    return dict(patches=patches, embed_weight=embed_weight, project_weight=project_weight, patch_counts=patch_counts, segment_ids=segment_ids, targets=targets)


def layer_norm(values):
    center = values - lax.optimization_barrier(jnp.mean(values, axis=-1, keepdims=True))
    spread = lax.optimization_barrier(jnp.mean(center * center, axis=-1, keepdims=True))
    return center * lax.rsqrt(spread + 1e-06)

def norm_grad(values, cotangent):
    return jax.vjp(layer_norm, values)[1](cotangent)[0]

def attend_block(query_raw, key_raw, value_rows, segment, target):
    inverse_root = 1.0 / math.sqrt(HD)
    query_normed = layer_norm(query_raw).astype(jnp.bfloat16)
    key_normed = layer_norm(key_raw).astype(jnp.bfloat16)
    scores = jnp.einsum('qhd,khd->hqk', query_normed.astype(jnp.float32), key_normed.astype(jnp.float32)) * inverse_root
    valid = segment >= 0
    allowed = (segment[:, None] == segment[None, :]) & valid[:, None]
    exponent = jnp.where(allowed[None], jnp.exp(scores), 0.0)
    denominator = lax.optimization_barrier(jnp.sum(exponent, axis=-1, keepdims=True))
    denominator = jnp.where(valid[None, :, None], denominator, 1.0)
    weights = (exponent / denominator).astype(jnp.bfloat16)
    attended = jnp.einsum('hqk,khd->qhd', weights.astype(jnp.float32), value_rows.astype(jnp.float32))
    feature_count = attended.shape[1] * attended.shape[2]
    error_rows = jnp.where(valid[:, None], attended.reshape(-1, feature_count) - target.astype(jnp.float32), 0.0)
    squared_sum = jnp.sum(error_rows * error_rows)
    return (query_normed, key_normed, weights, error_rows, squared_sum)

def attend_back(query_raw, key_raw, query_normed, key_normed, value_rows, weights, error_rows, patch_total):
    inverse_root = 1.0 / math.sqrt(HD)
    out_grad = (error_rows / patch_total).astype(jnp.bfloat16).reshape(query_normed.shape)
    prob_grad = jnp.einsum('qhd,khd->hqk', out_grad.astype(jnp.float32), value_rows.astype(jnp.float32))
    value_grad = jnp.einsum('hqk,qhd->khd', weights.astype(jnp.float32), out_grad.astype(jnp.float32)).astype(jnp.bfloat16)
    weight_float = weights.astype(jnp.float32)
    score_grad = (weight_float * (prob_grad - lax.optimization_barrier(jnp.sum(prob_grad * weight_float, axis=-1, keepdims=True))) * inverse_root).astype(jnp.bfloat16)
    normed_grad_q = jnp.einsum('hqk,khd->qhd', score_grad.astype(jnp.float32), key_normed.astype(jnp.float32))
    normed_grad_k = jnp.einsum('hqk,qhd->khd', score_grad.astype(jnp.float32), query_normed.astype(jnp.float32))
    query_grad = norm_grad(query_raw, normed_grad_q).astype(jnp.bfloat16)
    key_grad = norm_grad(key_raw, normed_grad_k).astype(jnp.bfloat16)
    return jnp.stack([query_grad, key_grad, value_grad], axis=1)

def reference(patches, embed_weight, project_weight, patch_counts, segment_ids, targets):
    embedded = jnp.dot(patches, embed_weight.T, preferred_element_type=jnp.float32).astype(jnp.bfloat16)
    normed = layer_norm(embedded.astype(jnp.float32)).astype(jnp.bfloat16)
    flat_weight = project_weight.reshape(D, 3 * HEADS * HD)
    projected = jnp.dot(normed, flat_weight, preferred_element_type=jnp.float32).reshape(N_DP, CAP, 3, HEADS, HD)
    patch_total = jnp.sum(patch_counts).astype(jnp.float32)
    segments = segment_ids.reshape(N_DP, CAP)
    target_blocks = targets.reshape(N_DP, CAP, HEADS * HD)

    def per_device(block_item):
        block_data, segment, target = block_item
        query_raw = block_data[:, 0]
        key_raw = block_data[:, 1]
        value_rows = block_data[:, 2].astype(jnp.bfloat16)
        query_normed, key_normed, weights, error_rows, squared_sum = attend_block(query_raw, key_raw, value_rows, segment, target)
        row_grads = attend_back(query_raw, key_raw, query_normed, key_normed, value_rows, weights, error_rows, patch_total)
        return (row_grads, squared_sum)
    row_grads, squared_sums = lax.map(per_device, (projected, segments, target_blocks))
    loss_value = jnp.sum(squared_sums) / (2.0 * patch_total)
    grad_rows = row_grads.reshape(N_DP * CAP, 3 * HEADS * HD)
    project_grad = jnp.dot(normed.T, grad_rows, preferred_element_type=jnp.float32).reshape(D, 3, HEADS * HD)
    return (project_grad, loss_value)
```

```python
import functools
import math

import jax
import jax.numpy as jnp
from jax import lax
from jax.experimental import pallas as pl
from jax.experimental.pallas import tpu as pltpu
from jax.sharding import PartitionSpec as P

HD = 128
KEEP = 96
MOVE = 64
PAD_P = 640


def layer_norm(values):
    center = values - jnp.mean(values, axis=-1, keepdims=True)
    spread = jnp.mean(center * center, axis=-1, keepdims=True)
    return center * lax.rsqrt(spread + 1e-06)


def norm_grad(values, cotangent):
    return jax.vjp(layer_norm, values)[1](cotangent)[0]


def attend_block(query_raw, key_raw, value_rows, segment, target):
    inverse_root = 1.0 / math.sqrt(HD)
    query_normed = layer_norm(query_raw).astype(jnp.bfloat16)
    key_normed = layer_norm(key_raw).astype(jnp.bfloat16)
    scores = (
        jnp.einsum("qhd,khd->hqk", query_normed, key_normed, preferred_element_type=jnp.float32)
        * inverse_root
    )
    valid = segment >= 0
    allowed = (segment[:, None] == segment[None, :]) & valid[:, None]
    exponent = jnp.where(allowed[None], jnp.exp(scores), 0.0)
    denominator = jnp.sum(exponent, axis=-1, keepdims=True)
    denominator = jnp.where(valid[None, :, None], denominator, 1.0)
    weights = (exponent / denominator).astype(jnp.bfloat16)
    attended = jnp.einsum("hqk,khd->qhd", weights, value_rows, preferred_element_type=jnp.float32)
    feature_count = attended.shape[1] * attended.shape[2]
    error_rows = jnp.where(
        valid[:, None], attended.reshape(-1, feature_count) - target.astype(jnp.float32), 0.0
    )
    squared_sum = jnp.sum(error_rows * error_rows)
    return (query_normed, key_normed, weights, error_rows, squared_sum)


def attend_back(
    query_raw, key_raw, query_normed, key_normed, value_rows, weights, error_rows, patch_total
):
    inverse_root = 1.0 / math.sqrt(HD)
    out_grad = (error_rows / patch_total).astype(jnp.bfloat16).reshape(query_normed.shape)
    prob_grad = jnp.einsum("qhd,khd->hqk", out_grad, value_rows, preferred_element_type=jnp.float32)
    value_grad = jnp.einsum(
        "hqk,qhd->khd", weights, out_grad, preferred_element_type=jnp.float32
    ).astype(jnp.bfloat16)
    weight_float = weights.astype(jnp.float32)
    score_grad = (
        weight_float
        * (prob_grad - jnp.sum(prob_grad * weight_float, axis=-1, keepdims=True))
        * inverse_root
    ).astype(jnp.bfloat16)
    normed_grad_q = jnp.einsum(
        "hqk,khd->qhd", score_grad, key_normed, preferred_element_type=jnp.float32
    )
    normed_grad_k = jnp.einsum(
        "hqk,qhd->khd", score_grad, query_normed, preferred_element_type=jnp.float32
    )
    query_grad = norm_grad(query_raw, normed_grad_q).astype(jnp.bfloat16)
    key_grad = norm_grad(key_raw, normed_grad_k).astype(jnp.bfloat16)
    return jnp.stack([query_grad, key_grad, value_grad], axis=1)


def shift(array, axis, size, step):
    return lax.ppermute(array, axis, [(i, (i + step) % size) for i in range(size)])


def balance(patches, targets, segment_ids, patch_counts, n_dp):
    ends = jnp.cumsum(patch_counts)
    own = jnp.max(jnp.where(ends <= KEEP, ends, 0))
    feats = patches.shape[1] + targets.shape[1] + 1
    width = -(-feats // 128) * 128
    rows = jnp.concatenate(
        [
            patches,
            targets,
            (segment_ids + 1).astype(jnp.bfloat16)[:, None],
            jnp.zeros((patches.shape[0], width - feats), jnp.bfloat16),
        ],
        axis=1,
    )
    padded = jnp.concatenate([rows, jnp.zeros((MOVE, width), jnp.bfloat16)], axis=0)
    leaving = lax.dynamic_slice(padded, (own, 0), (MOVE, width))
    half = n_dp // 2
    coming = lax.ppermute(leaving, "dp", [(i + half, i) for i in range(half)])
    around = jnp.concatenate(
        [
            jnp.zeros((KEEP, width), jnp.bfloat16),
            coming,
            jnp.zeros((KEEP - MOVE, width), jnp.bfloat16),
        ],
        axis=0,
    )
    placed = lax.dynamic_slice(around, (KEEP - own, 0), (KEEP, width))
    keep = jnp.arange(KEEP)[:, None] < own
    merged = jnp.where(keep, rows[:KEEP], placed)
    p_size, t_size = patches.shape[1], targets.shape[1]
    segment = merged[:, p_size + t_size].astype(jnp.int32) - 1
    return merged[:, :p_size], merged[:, p_size : p_size + t_size], segment


def norm_kernel(me_ref, *refs):
    blocks, out_ref = refs[:-1], refs[-1]
    me = me_ref[0]
    count = 8
    width = blocks[0].shape[1]
    values = [b[...].astype(jnp.float32) for b in blocks[:-2]]
    far = jnp.concatenate([blocks[-2][...], blocks[-1][...]], axis=0).astype(jnp.float32)
    values.append(far)
    offsets = [0]
    for step in range(1, count // 2):
        offsets += [-step, step]
    offsets.append(count // 2)
    features = width * count
    total = sum(jnp.sum(v, axis=1, keepdims=True) for v in values)
    mean = total / features
    spread = sum(jnp.sum((v - mean) * (v - mean), axis=1, keepdims=True) for v in values)
    scale = lax.rsqrt(spread / features + 1e-06)
    for offset, v in zip(offsets, values):
        place = lax.rem(me + offset + count, count)
        out_ref[:, pl.ds(pl.multiple_of(place * width, 128), width)] = (
            (v - mean) * scale
        ).astype(jnp.bfloat16)


def gather_norm(own, me, n_mp):
    blocks = [own]
    ahead = back = own
    for _ in range(1, n_mp // 2):
        ahead = shift(ahead, "mp", n_mp, 1)
        back = shift(back, "mp", n_mp, -1)
        blocks += [ahead, back]
    half = own.shape[0] // 2
    blocks.append(shift(ahead[:half], "mp", n_mp, 1))
    blocks.append(shift(back[half:], "mp", n_mp, -1))
    return pl.pallas_call(
        norm_kernel,
        out_shape=jax.ShapeDtypeStruct((own.shape[0], own.shape[1] * n_mp), jnp.bfloat16),
        in_specs=[pl.BlockSpec(memory_space=pltpu.SMEM)]
        + [pl.BlockSpec(memory_space=pltpu.VMEM)] * len(blocks),
        out_specs=pl.BlockSpec(memory_space=pltpu.VMEM),
        compiler_params=pltpu.CompilerParams(vmem_limit_bytes=40 * 1024 * 1024),
        cost_estimate=pl.CostEstimate(flops=4_000_000, bytes_accessed=2_400_000, transcendentals=0),
    )(me.reshape(1), *blocks)


def local(n_dp, n_mp, patches, embed_weight, project_weight, patch_counts, segment_ids, targets):
    flat_weight = project_weight.reshape(project_weight.shape[0], -1)
    whole_weight = lax.all_gather(flat_weight, "dp", axis=0, tiled=True)

    p_size = patches.shape[1]
    local_total = jnp.sum(patch_counts).astype(jnp.bfloat16)
    extra = jnp.zeros((embed_weight.shape[0], PAD_P - p_size), jnp.bfloat16)
    extra = extra.at[0, 0].set(local_total)
    wide = lax.all_gather(
        jnp.concatenate([embed_weight, extra], axis=1), "dp", axis=0, tiled=True
    )
    patch_total = jnp.sum(wide[:, p_size].astype(jnp.float32))
    patches, targets, segment_ids = balance(patches, targets, segment_ids, patch_counts, n_dp)
    row_total = patches.shape[0]
    padded = jnp.concatenate(
        [patches, jnp.zeros((row_total, PAD_P - p_size), jnp.bfloat16)], axis=1
    )
    own_features = jnp.einsum(
        "rp,cp->rc", padded, wide, preferred_element_type=jnp.float32
    ).astype(jnp.bfloat16)
    normed = gather_norm(own_features, lax.axis_index("mp"), n_mp)
    projected = jnp.dot(normed, whole_weight, preferred_element_type=jnp.float32)
    head_dev = project_weight.shape[2] // HD
    projected = projected.reshape(row_total, 3, head_dev, HD)
    query_raw = projected[:, 0]
    key_raw = projected[:, 1]
    value_rows = projected[:, 2].astype(jnp.bfloat16)
    query_normed, key_normed, weights, error_rows, squared_sum = attend_block(
        query_raw, key_raw, value_rows, segment_ids, targets
    )
    grad_rows = attend_back(
        query_raw, key_raw, query_normed, key_normed, value_rows, weights, error_rows, patch_total
    )
    grad_rows = grad_rows.reshape(row_total, -1)
    all_grads = lax.all_gather(grad_rows, "dp", axis=0, tiled=True)
    normed_blocks = lax.all_to_all(normed, "dp", split_axis=1, concat_axis=0, tiled=True)
    squared_mp = lax.psum(squared_sum, "mp")
    squared_tile = lax.optimization_barrier(jnp.broadcast_to(squared_mp, (8, 128)))
    squared_tiles = lax.all_gather(squared_tile, "dp", axis=0, tiled=True)
    squared_all = jnp.sum(lax.optimization_barrier(squared_tiles)[::8, 0])
    loss_value = squared_all / (2.0 * patch_total)
    weight_grad = lax.dot_general(
        normed_blocks,
        all_grads,
        (((0,), (0,)), ((), ())),
        preferred_element_type=jnp.float32,
    )
    return (weight_grad.reshape(weight_grad.shape[0], 3, -1), loss_value)


def solution(mesh):
    in_specs = (
        P("dp", None),
        P(("mp", "dp"), None),
        P("dp", None, "mp"),
        P("dp"),
        P("dp"),
        P("dp", "mp"),
    )
    out_specs = (P("dp", None, "mp"), P())
    sizes = mesh.shape
    return jax.shard_map(
        functools.partial(local, sizes["dp"], sizes["mp"]),
        mesh=mesh,
        in_specs=in_specs,
        out_specs=out_specs,
        check_vma=False,
    )
```

```python
import functools
import math

import jax
import jax.numpy as jnp
from jax import lax
from jax.experimental import pallas as pl
from jax.experimental.pallas import tpu as pltpu
from jax.sharding import Mesh
from jax.sharding import PartitionSpec as P

HD = 128
KEEP = 96
MOVE = 64
P_SIZE = 588
PAD_P = 640
SHARE = 16
SHARES = KEEP // SHARE
STATS = 16
SEGMENT = 600
SIDE = 4
CHIPS = 16
CORES = 2
N_MP = 8
DP = ("y", "x", "core")
F32 = jnp.float32
BF16 = jnp.bfloat16
VMEM = pl.BlockSpec(memory_space=pltpu.VMEM)
SMEM = pl.BlockSpec(memory_space=pltpu.SMEM)
ROOM = pltpu.CompilerParams(vmem_limit_bytes=48 * 1024 * 1024)


def shift(array, axis, size, step):
    return lax.ppermute(array, axis, [(i, (i + step) % size) for i in range(size)])


def swap(array):
    return lax.ppermute(array, "core", [(0, 1), (1, 0)])


def turn(array, first, step):
    pairs = []
    for y in range(SIDE):
        for x in range(SIDE):
            for core in range(CORES):
                along_x = (core == 0) == first
                to_y = y if along_x else (y + step) % SIDE
                to_x = (x + step) % SIDE if along_x else x
                pairs.append(((y * SIDE + x) * CORES + core, (to_y * SIDE + to_x) * CORES + core))
    return lax.ppermute(array, DP, pairs)


def rows_kept(counts_ref):
    end = jnp.int32(0)
    kept = jnp.int32(0)
    for slot in range(counts_ref.shape[0]):
        end = end + counts_ref[slot]
        kept = jnp.where(end <= KEEP, end, kept)
    return pl.multiple_of(kept, 16), end


def pack_kernel(counts_ref, patch_ref, target_ref, segment_ref, embed_ref, all_ref, leave_ref, wide_ref, tall):
    p_size, rows = patch_ref.shape
    tall[...] = jnp.zeros_like(tall)
    tall[:p_size, :] = patch_ref[...].astype(F32)
    marks = jnp.broadcast_to(segment_ref[...].astype(F32) + 1.0, (8, rows))
    tall[SEGMENT : SEGMENT + 8, :] = marks
    all_ref[:rows, :PAD_P] = tall[...].T.astype(BF16)
    all_ref[:rows, PAD_P:] = target_ref[...]
    all_ref[rows:, :] = jnp.zeros((all_ref.shape[0] - rows, all_ref.shape[1]), BF16)
    kept, total = rows_kept(counts_ref)
    leave_ref[...] = all_ref[pl.ds(kept, MOVE), :]
    row = lax.broadcasted_iota(jnp.int32, (wide_ref.shape[0], wide_ref.shape[1] - 512), 0)
    column = lax.broadcasted_iota(jnp.int32, (wide_ref.shape[0], wide_ref.shape[1] - 512), 1)
    here = (row == 0) & (column == p_size - 512)
    wide_ref[:, 512:] = jnp.where(here, total.astype(F32), 0.0).astype(BF16)
    wide_ref[:, :p_size] = embed_ref[...]


def pack(patches, targets, segment_ids, patch_counts, embed_weight):
    rows, p_size = patches.shape
    width = PAD_P + targets.shape[1]
    return pl.pallas_call(
        pack_kernel,
        out_shape=(
            jax.ShapeDtypeStruct((rows + MOVE, width), BF16),
            jax.ShapeDtypeStruct((MOVE, width), BF16),
            jax.ShapeDtypeStruct((embed_weight.shape[0], PAD_P), BF16),
        ),
        grid=(1,),
        in_specs=[SMEM]
        + [
            pl.BlockSpec(shape, lambda i: (0, 0))
            for shape in ((p_size, rows), targets.shape, (1, rows), embed_weight.shape)
        ],
        out_specs=tuple(
            pl.BlockSpec(shape, lambda i: (0, 0))
            for shape in ((rows + MOVE, width), (MOVE, width), (embed_weight.shape[0], PAD_P))
        ),
        scratch_shapes=[pltpu.VMEM((PAD_P, rows), F32)],
        compiler_params=ROOM,
        cost_estimate=pl.CostEstimate(flops=1_000_000, bytes_accessed=1_000_000, transcendentals=0),
    )(patch_counts, patches.T, targets, segment_ids.reshape(1, rows), embed_weight)


def embed_kernel(counts_ref, all_ref, come_ref, wide_ref, out_ref, target_ref, column_ref, row_ref, total_ref, around):
    kept, _ = rows_kept(counts_ref)
    around[...] = jnp.zeros_like(around)
    around[pl.ds(kept, MOVE), :] = come_ref[...]
    mine = lax.broadcasted_iota(jnp.int32, (KEEP, 1), 0) < kept
    merged = jnp.where(mine, all_ref[:KEEP, :], around[:KEEP, :])
    target_ref[...] = merged[:, PAD_P:]
    marks = merged[:, PAD_P - 128 : PAD_P].astype(F32)
    slot = lax.broadcasted_iota(jnp.int32, marks.shape, 1) == SEGMENT - (PAD_P - 128)
    mark = jnp.sum(jnp.where(slot, marks, 0.0), axis=1, keepdims=True) - 1.0
    spread = jnp.broadcast_to(mark, marks.shape)
    column_ref[...] = spread.astype(jnp.int32)
    row_ref[...] = spread.T[:8, :].astype(jnp.int32)
    tail = wide_ref[:, PAD_P - 128 : PAD_P].astype(F32)
    slot = lax.broadcasted_iota(jnp.int32, tail.shape, 1) == P_SIZE - (PAD_P - 128)
    total_ref[...] = jnp.full(total_ref.shape, jnp.sum(jnp.where(slot, tail, 0.0)), F32)
    out_ref[...] = dot_t(merged[:, :PAD_P], wide_ref[...]).astype(BF16)


def embed(patch_counts, packed, coming, wide):
    targets = packed.shape[1] - PAD_P
    return pl.pallas_call(
        embed_kernel,
        out_shape=(
            jax.ShapeDtypeStruct((KEEP, wide.shape[0]), BF16),
            jax.ShapeDtypeStruct((KEEP, targets), BF16),
            jax.ShapeDtypeStruct((KEEP, 128), jnp.int32),
            jax.ShapeDtypeStruct((8, KEEP), jnp.int32),
            jax.ShapeDtypeStruct((8, 128), F32),
        ),
        in_specs=[SMEM] + [VMEM] * 3,
        out_specs=(VMEM,) * 5,
        scratch_shapes=[pltpu.VMEM((KEEP + MOVE, packed.shape[1]), BF16)],
        compiler_params=ROOM,
        cost_estimate=pl.CostEstimate(
            flops=100_000_000, bytes_accessed=2_000_000, transcendentals=0
        ),
    )(patch_counts, packed, coming, wide)


def by_parity(values):
    part = [values[:, 128 * i : 128 * (i + 1)] for i in range(6)]
    turned = [pltpu.roll(p, 64, 1) for p in part]
    low = lax.broadcasted_iota(jnp.int32, part[0].shape, 1) < 64
    even = [part[0], jnp.where(low, part[1], turned[3]), jnp.where(low, turned[3], turned[4])]
    odd = [jnp.where(low, turned[1], turned[2]), jnp.where(low, turned[2], part[4]), part[5]]
    return jnp.concatenate(even, axis=1), jnp.concatenate(odd, axis=1)


def norm_kernel(place_ref, *refs):
    blocks, (share_ref, own_ref, other_ref, chips_ref) = refs[:-4], refs[-4:]
    me, core = place_ref[0], place_ref[1]
    width = blocks[0].shape[1]
    values = [b[...].astype(F32) for b in blocks[:-2]]
    values.append(jnp.concatenate([blocks[-2][...], blocks[-1][...]], axis=0).astype(F32))
    offsets = [0]
    for step in range(1, N_MP // 2):
        offsets += [-step, step]
    offsets.append(N_MP // 2)
    features = width * N_MP
    mean = sum(jnp.sum(v, axis=1, keepdims=True) for v in values) / features
    spread = sum(jnp.sum((v - mean) * (v - mean), axis=1, keepdims=True) for v in values)
    scale = lax.rsqrt(spread / features + 1e-06)
    half = width // 2
    for offset, v in zip(offsets, values):
        place = lax.rem(me + offset + N_MP, N_MP)
        normed = (v - mean) * scale
        chips_ref[2 * place] = normed[:, :half].astype(BF16)
        chips_ref[2 * place + 1] = normed[:, half:].astype(BF16)
        even, odd = by_parity(normed)
        first = core == 0
        columns = pl.ds(pl.multiple_of(place * half, 128), half)
        own_ref[:, columns] = jnp.where(first, even, odd).astype(BF16)
        other_ref[:, columns] = jnp.where(first, odd, even).astype(BF16)
    start = pl.multiple_of(jnp.minimum(me, SHARES - 1) * SHARE, SHARE)
    share_ref[...] = chips_ref[:, pl.ds(start, SHARE), :]


def gather_norm(own, place):
    blocks = [own]
    ahead = back = own
    for _ in range(1, N_MP // 2):
        ahead = shift(ahead, "mp", N_MP, 1)
        back = shift(back, "mp", N_MP, -1)
        blocks += [ahead, back]
    half = own.shape[0] // 2
    blocks.append(shift(ahead[:half], "mp", N_MP, 1))
    blocks.append(shift(back[half:], "mp", N_MP, -1))
    rows, width = own.shape
    return pl.pallas_call(
        norm_kernel,
        out_shape=(
            jax.ShapeDtypeStruct((2 * N_MP, SHARE, width // 2), BF16),
            jax.ShapeDtypeStruct((rows, width * N_MP // 2), BF16),
            jax.ShapeDtypeStruct((rows, width * N_MP // 2), BF16),
        ),
        in_specs=[SMEM] + [VMEM] * len(blocks),
        out_specs=(VMEM, VMEM, VMEM),
        scratch_shapes=[pltpu.VMEM((2 * N_MP, rows, width // 2), BF16)],
        compiler_params=ROOM,
        cost_estimate=pl.CostEstimate(flops=4_000_000, bytes_accessed=4_000_000, transcendentals=0),
    )(place, *blocks)


def project_kernel(own_ref, other_ref, weight_ref, own_out, other_out):
    @pl.when(pl.program_id(0) == 0)
    def _():
        own_out[...] = jnp.zeros_like(own_out)
        other_out[...] = jnp.zeros_like(other_out)

    rows = own_ref.shape[0]
    chips, groups = weight_ref.shape[:2]
    left = jnp.concatenate([own_ref[...], other_ref[...]], axis=0)
    right = jnp.concatenate(
        [
            jnp.concatenate([weight_ref[i, group] for group in range(groups)], axis=1)
            for i in range(chips)
        ],
        axis=0,
    )
    product = jnp.dot(left, right, preferred_element_type=F32)
    own_out[...] += product[:rows]
    other_out[...] += product[rows:]


def project(own, other, weight):
    rows = own.shape[0]
    chips, groups, depth, span = weight.shape
    step = 4
    block = pl.BlockSpec((rows, step * depth), lambda i: (0, i))
    result = pl.BlockSpec((rows, groups * span), lambda i: (0, 0))
    return pl.pallas_call(
        project_kernel,
        grid=(chips // step,),
        out_shape=(jax.ShapeDtypeStruct((rows, groups * span), F32),) * 2,
        in_specs=[
            block,
            block,
            pl.BlockSpec((step, groups, depth, span), lambda i: (i, 0, 0, 0)),
        ],
        out_specs=(result, result),
        compiler_params=ROOM,
        cost_estimate=pl.CostEstimate(
            flops=1_360_000_000, bytes_accessed=9_000_000, transcendentals=0
        ),
    )(own, other, weight)


def dot_t(a, b):
    return lax.dot_general(a, b, (((1,), (1,)), ((), ())), preferred_element_type=F32)


def t_dot(a, b):
    return lax.dot_general(a, b, (((0,), (0,)), ((), ())), preferred_element_type=F32)


def norm_parts(values):
    center = values - jnp.mean(values, axis=-1, keepdims=True)
    scale = lax.rsqrt(jnp.mean(center * center, axis=-1, keepdims=True) + 1e-06)
    return center * scale, scale


def norm_grad(normed, scale, cotangent):
    along = jnp.mean(cotangent * normed, axis=-1, keepdims=True)
    return scale * (cotangent - jnp.mean(cotangent, axis=-1, keepdims=True) - normed * along)


def attend_kernel(raw_ref, more_ref, row_ref, column_ref, target_ref, total_ref, grad_ref):
    inverse_root = 1.0 / math.sqrt(HD)
    heads = target_ref.shape[1] // HD
    rows = raw_ref.shape[0]
    row_segment = row_ref[:, :1]
    valid = row_segment >= 0
    allowed = (row_segment == column_ref[:1, :]) & valid
    total = total_ref[:1, :1]
    squares = jnp.zeros((raw_ref.shape[0], HD), F32)
    for head in range(heads):
        cut = [slice((part * heads + head) * HD, (part * heads + head + 1) * HD) for part in range(3)]
        query, key, value = [raw_ref[:, c] + more_ref[:, c] for c in cut]
        query_exact, query_scale = norm_parts(query)
        key_exact, key_scale = norm_parts(key)
        query_normed = query_exact.astype(BF16)
        key_normed = key_exact.astype(BF16)
        value_rows = value.astype(BF16)
        scores = dot_t(query_normed, key_normed) * inverse_root
        exponent = jnp.where(allowed, jnp.exp(scores), 0.0)
        denominator = jnp.sum(exponent, axis=-1, keepdims=True)
        denominator = jnp.where(valid, denominator, 1.0)
        weights = (exponent / denominator).astype(BF16)
        attended = jnp.dot(weights, value_rows, preferred_element_type=F32)
        target = target_ref[:, head * HD : (head + 1) * HD].astype(F32)
        error = jnp.where(valid, attended - target, 0.0)
        squares += error * error
        out_grad = (error / total).astype(BF16)
        prob_grad = dot_t(out_grad, value_rows)
        grad_ref[:rows, cut[2]] = t_dot(weights, out_grad).astype(BF16)
        weight_float = weights.astype(F32)
        inner = jnp.sum(prob_grad * weight_float, axis=-1, keepdims=True)
        score_grad = (weight_float * (prob_grad - inner) * inverse_root).astype(BF16)
        query_cotangent = jnp.dot(score_grad, key_normed, preferred_element_type=F32)
        key_cotangent = t_dot(score_grad, query_normed)
        grad_ref[:rows, cut[0]] = norm_grad(query_exact, query_scale, query_cotangent).astype(BF16)
        grad_ref[:rows, cut[1]] = norm_grad(key_exact, key_scale, key_cotangent).astype(BF16)
    square = jnp.full((STATS, grad_ref.shape[1]), jnp.sum(squares), F32)
    high = square.astype(BF16).astype(F32)
    middle = (square - high).astype(BF16).astype(F32)
    low = square - high - middle
    place = lax.broadcasted_iota(jnp.int32, square.shape, 0)
    terms = jnp.where(place == 0, high, jnp.where(place == 1, middle, low))
    grad_ref[rows:, :] = jnp.where(place < 3, terms, 0.0).astype(BF16)


def attend(raw, more, column, row, targets, patch_total):
    rows, width = raw.shape
    return pl.pallas_call(
        attend_kernel,
        out_shape=jax.ShapeDtypeStruct((rows + STATS, width), BF16),
        in_specs=[VMEM] * 6,
        out_specs=VMEM,
        compiler_params=ROOM,
        cost_estimate=pl.CostEstimate(
            flops=50_000_000, bytes_accessed=1_500_000, transcendentals=30_000
        ),
    )(raw, more, column, row, targets, patch_total)


def turn_kernel(place_ref, blocks_ref, own_ref, other_ref):
    y, x, core = place_ref[0], place_ref[1], place_ref[2]
    half = blocks_ref.shape[3] // 2
    rows = SHARES * SHARE
    ring = (0, -1, 1, 2)
    pieces = []
    for far in ring:
        for near in ring:
            step_x = jnp.where(core == 0, near, far)
            step_y = jnp.where(core == 0, far, near)
            chip = lax.rem(y + step_y + SIDE, SIDE) * SIDE + lax.rem(x + step_x + SIDE, SIDE)
            pieces += [blocks_ref[share, chip] for share in range(SHARES)]
    for group in range(SIDE):
        several = pieces[group * SIDE * SHARES : (group + 1) * SIDE * SHARES]
        wide = jnp.concatenate(several, axis=0).astype(F32).T.astype(BF16)
        columns = slice(group * SIDE * rows, (group + 1) * SIDE * rows)
        first = core == 0
        own_ref[:, columns] = jnp.where(first, wide[:half], wide[half:])
        other_ref[:, columns] = jnp.where(first, wide[half:], wide[:half])


def turn_blocks(blocks, place):
    _, chips, _, feats = blocks.shape
    return pl.pallas_call(
        turn_kernel,
        out_shape=(jax.ShapeDtypeStruct((feats // 2, chips * KEEP), BF16),) * 2,
        in_specs=[SMEM, VMEM],
        out_specs=(VMEM, VMEM),
        compiler_params=ROOM,
        cost_estimate=pl.CostEstimate(flops=1_000_000, bytes_accessed=2_400_000, transcendentals=0),
    )(place, blocks)


def grad_kernel(parts, own_ref, other_ref, *refs):
    pieces, (own_out, other_out) = refs[:parts], refs[parts:]
    for left_ref, out_ref in ((other_ref, other_out), (own_ref, own_out)):
        groups, _, span = out_ref.shape
        total = None
        start = 0
        for piece in pieces:
            rows = piece.shape[0]
            product = jnp.dot(
                left_ref[:, start : start + rows], piece[...], preferred_element_type=F32
            )
            total = product if total is None else total + product
            start += rows
        for group in range(groups):
            out_ref[group] = total[:, group * span : (group + 1) * span]


def grad_first(own, other, pieces, groups):
    width = pieces[0].shape[1]
    part = jax.ShapeDtypeStruct((groups, own.shape[0], width // groups), F32)
    return pl.pallas_call(
        functools.partial(grad_kernel, len(pieces)),
        out_shape=(part, part),
        in_specs=[VMEM] * (2 + len(pieces)),
        out_specs=(VMEM, VMEM),
        compiler_params=ROOM,
        cost_estimate=pl.CostEstimate(
            flops=1_000_000_000, bytes_accessed=5_000_000, transcendentals=0
        ),
    )(own, other, *pieces)


def last_kernel(start, left_ref, piece_ref, part_ref, out_ref):
    rows = piece_ref.shape[0]
    product = jnp.dot(
        left_ref[:, start : start + rows], piece_ref[...], preferred_element_type=F32
    )
    groups, _, span = out_ref.shape
    for group in range(groups):
        out_ref[group] = part_ref[group] + product[:, group * span : (group + 1) * span]


def grad_last(left, piece, part):
    return pl.pallas_call(
        functools.partial(last_kernel, left.shape[1] - piece.shape[0]),
        out_shape=jax.ShapeDtypeStruct(part.shape, F32),
        in_specs=[VMEM] * 3,
        out_specs=VMEM,
        compiler_params=ROOM,
        cost_estimate=pl.CostEstimate(
            flops=170_000_000, bytes_accessed=3_000_000, transcendentals=0
        ),
    )(left, piece, part)


def add_kernel(a_ref, b_ref, out_ref):
    out_ref[...] = a_ref[...] + b_ref[...]


def add(a, b):
    return pl.pallas_call(
        add_kernel,
        out_shape=jax.ShapeDtypeStruct(a.shape, F32),
        in_specs=[VMEM, VMEM],
        out_specs=VMEM,
        compiler_params=ROOM,
    )(a, b)


def near_kernel(*refs):
    blocks, (out_ref, sum_ref) = refs[:-2], refs[-2:]
    rows = blocks[0].shape[0] - STATS
    terms = 0.0
    for index, block in enumerate(blocks):
        out_ref[index * rows : (index + 1) * rows, :] = block[:rows, :]
        terms += block[rows:, :128].astype(F32)
    sum_ref[...] = jnp.broadcast_to(jnp.sum(terms, axis=0, keepdims=True), sum_ref.shape)


def near_rows(blocks):
    rows, width = blocks[0].shape
    return pl.pallas_call(
        near_kernel,
        out_shape=(
            jax.ShapeDtypeStruct((len(blocks) * (rows - STATS), width), BF16),
            jax.ShapeDtypeStruct((8, 128), F32),
        ),
        in_specs=[VMEM] * len(blocks),
        out_specs=(VMEM, VMEM),
        compiler_params=ROOM,
        cost_estimate=pl.CostEstimate(flops=100_000, bytes_accessed=1_800_000, transcendentals=0),
    )(*blocks)


def local(patches, embed_weight, project_weight, patch_counts, segment_ids, targets):
    whole_weight = lax.all_gather(project_weight.transpose(1, 0, 2), ("y", "x"), axis=0)
    y, x, core, mp = [lax.axis_index(a) for a in ("y", "x", "core", "mp")]

    packed, leaving, embed_part = pack(patches, targets, segment_ids, patch_counts, embed_weight)
    half = CHIPS * CORES // 2
    coming = lax.ppermute(leaving, DP, [(i + half, i) for i in range(half)])
    wide = lax.all_gather(embed_part, DP, axis=0, tiled=True)
    own_features, targets, column, row, total_tile = embed(patch_counts, packed, coming, wide)
    chip_blocks, own_half, other_half = gather_norm(own_features, jnp.stack([mp, core]))
    chip_share = lax.all_to_all(chip_blocks, ("y", "x"), split_axis=0, concat_axis=0, tiled=True)
    more_half, chip_share = lax.optimization_barrier((swap(other_half), chip_share))
    chip_rows = lax.all_gather(chip_share, "mp", axis=0)
    own_part, other_part = project(own_half, more_half, whole_weight)
    grad_rows = attend(own_part, swap(other_part), column, row, targets, total_tile)

    behind, ahead = lax.optimization_barrier(
        (turn(grad_rows, True, 1), turn(grad_rows, True, -1))
    )
    near, tile = near_rows([grad_rows, behind, ahead, turn(behind, True, 1)])
    own_left, other_left = turn_blocks(chip_rows, jnp.stack([y, x, core]))
    behind, ahead = turn(near, False, 1), turn(near, False, -1)
    for step in (1, 2, 4):
        tile = tile + shift(tile, "mp", N_MP, step)
    behind, ahead, tile, own_left, other_left = lax.optimization_barrier(
        (behind, ahead, tile, own_left, other_left)
    )
    groups = project_weight.shape[1]
    own_grad, other_grad = grad_first(own_left, other_left, (near, behind, ahead), groups)
    opposite = turn(behind, False, 1)
    for step in (-1, -2):
        tile = tile + turn(tile, False, step)
    opposite, tile, own_grad, other_grad = lax.optimization_barrier(
        (opposite, tile, own_grad, other_grad)
    )
    more_grad, more_tile = lax.optimization_barrier(
        (swap(grad_last(other_left, opposite, other_grad)), swap(tile))
    )
    weight_grad = add(grad_last(own_left, opposite, own_grad), more_grad)
    loss_value = (tile + more_tile)[0, 0] / (2.0 * total_tile[0, 0])
    return (weight_grad.transpose(1, 0, 2), loss_value)


def solution(mesh):
    chips = Mesh(mesh.devices.reshape(SIDE, SIDE, CORES, N_MP), DP + ("mp",))
    in_specs = (
        P(DP, None),
        P(("mp",) + DP, None),
        P(DP, None, "mp"),
        P(DP),
        P(DP),
        P(DP, "mp"),
    )
    out_specs = (P(DP, None, "mp"), P())
    return jax.shard_map(
        local, mesh=chips, in_specs=in_specs, out_specs=out_specs, check_vma=False
    )
```

```python
import functools
import math

import jax
import jax.numpy as jnp
from jax import lax
from jax.experimental import pallas as pl
from jax.experimental.pallas import tpu as pltpu
from jax.sharding import Mesh
from jax.sharding import PartitionSpec as P

HD = 128
KEEP = 96
MOVE = 64
P_SIZE = 588
PAD_P = 640
SHARE = 16
SHARES = KEEP // SHARE
STATS = 16
SEGMENT = 600
SIDE = 4
CHIPS = 16
CORES = 2
N_MP = 8
DP = ("y", "x", "core")
F32 = jnp.float32
BF16 = jnp.bfloat16
VMEM = pl.BlockSpec(memory_space=pltpu.VMEM)
SMEM = pl.BlockSpec(memory_space=pltpu.SMEM)
ROOM = pltpu.CompilerParams(vmem_limit_bytes=48 * 1024 * 1024)


def shift(array, axis, size, step):
    return lax.ppermute(array, axis, [(i, (i + step) % size) for i in range(size)])


def swap(array):
    return lax.ppermute(array, "core", [(0, 1), (1, 0)])


def turn(array, first, step):
    pairs = []
    for y in range(SIDE):
        for x in range(SIDE):
            for core in range(CORES):
                along_x = (core == 0) == first
                to_y = y if along_x else (y + step) % SIDE
                to_x = (x + step) % SIDE if along_x else x
                pairs.append(((y * SIDE + x) * CORES + core, (to_y * SIDE + to_x) * CORES + core))
    return lax.ppermute(array, DP, pairs)


def rows_kept(counts_ref):
    end = jnp.int32(0)
    kept = jnp.int32(0)
    for slot in range(counts_ref.shape[0]):
        end = end + counts_ref[slot]
        kept = jnp.where(end <= KEEP, end, kept)
    return pl.multiple_of(kept, 16), end


def pack_kernel(counts_ref, *refs):
    sources, (all_ref, leave_ref, wide_ref, tall), rest = refs[:4], refs[4:8], refs[8:]
    places, sem = rest[:4], rest[4]
    copies = [
        pltpu.make_async_copy(source, place, sem.at[index])
        for index, (source, place) in enumerate(zip(sources, places))
    ]
    for copy in copies:
        copy.start()
    for copy in copies:
        copy.wait()
    patch_ref, target_ref, segment_ref, embed_ref = places
    p_size, rows = patch_ref.shape
    tall[...] = jnp.zeros_like(tall)
    tall[:p_size, :] = patch_ref[...].astype(F32)
    marks = jnp.broadcast_to(segment_ref[...].astype(F32) + 1.0, (8, rows))
    tall[SEGMENT : SEGMENT + 8, :] = marks
    all_ref[:rows, :PAD_P] = tall[...].T.astype(BF16)
    all_ref[:rows, PAD_P:] = target_ref[...]
    all_ref[rows:, :] = jnp.zeros((all_ref.shape[0] - rows, all_ref.shape[1]), BF16)
    kept, total = rows_kept(counts_ref)
    leave_ref[...] = all_ref[pl.ds(kept, MOVE), :]
    row = lax.broadcasted_iota(jnp.int32, (wide_ref.shape[0], wide_ref.shape[1] - 512), 0)
    column = lax.broadcasted_iota(jnp.int32, (wide_ref.shape[0], wide_ref.shape[1] - 512), 1)
    here = (row == 0) & (column == p_size - 512)
    wide_ref[:, 512:] = jnp.where(here, total.astype(F32), 0.0).astype(BF16)
    wide_ref[:, :p_size] = embed_ref[...]


def pack(patches, targets, segment_ids, patch_counts, embed_weight):
    rows, p_size = patches.shape
    width = PAD_P + targets.shape[1]
    return pl.pallas_call(
        pack_kernel,
        out_shape=(
            jax.ShapeDtypeStruct((rows + MOVE, width), BF16),
            jax.ShapeDtypeStruct((MOVE, width), BF16),
            jax.ShapeDtypeStruct((embed_weight.shape[0], PAD_P), BF16),
        ),
        in_specs=[SMEM] + [pl.BlockSpec(memory_space=pltpu.HBM)] * 4,
        out_specs=(VMEM, VMEM, VMEM),
        scratch_shapes=[
            pltpu.VMEM((PAD_P, rows), F32),
            pltpu.VMEM((p_size, rows), BF16),
            pltpu.VMEM(targets.shape, BF16),
            pltpu.VMEM((1, rows), jnp.int32),
            pltpu.VMEM(embed_weight.shape, BF16),
            pltpu.SemaphoreType.DMA((4,)),
        ],
        cost_estimate=pl.CostEstimate(flops=1_000_000, bytes_accessed=1_000_000, transcendentals=0),
    )(patch_counts, patches.T, targets, segment_ids.reshape(1, rows), embed_weight)


def embed_kernel(counts_ref, all_ref, come_ref, wide_ref, out_ref, target_ref, column_ref, row_ref, total_ref, around):
    kept, _ = rows_kept(counts_ref)
    around[...] = jnp.zeros_like(around)
    around[pl.ds(kept, MOVE), :] = come_ref[...]
    mine = lax.broadcasted_iota(jnp.int32, (KEEP, 1), 0) < kept
    merged = jnp.where(mine, all_ref[:KEEP, :], around[:KEEP, :])
    target_ref[...] = merged[:, PAD_P:]
    marks = merged[:, PAD_P - 128 : PAD_P].astype(F32)
    slot = lax.broadcasted_iota(jnp.int32, marks.shape, 1) == SEGMENT - (PAD_P - 128)
    mark = jnp.sum(jnp.where(slot, marks, 0.0), axis=1, keepdims=True) - 1.0
    spread = jnp.broadcast_to(mark, marks.shape)
    column_ref[...] = spread.astype(jnp.int32)
    row_ref[...] = spread.T[:8, :].astype(jnp.int32)
    tail = wide_ref[:, PAD_P - 128 : PAD_P].astype(F32)
    slot = lax.broadcasted_iota(jnp.int32, tail.shape, 1) == P_SIZE - (PAD_P - 128)
    total_ref[...] = jnp.full(total_ref.shape, jnp.sum(jnp.where(slot, tail, 0.0)), F32)
    out_ref[...] = dot_t(merged[:, :PAD_P], wide_ref[...]).astype(BF16)


def embed(patch_counts, packed, coming, wide):
    targets = packed.shape[1] - PAD_P
    return pl.pallas_call(
        embed_kernel,
        out_shape=(
            jax.ShapeDtypeStruct((KEEP, wide.shape[0]), BF16),
            jax.ShapeDtypeStruct((KEEP, targets), BF16),
            jax.ShapeDtypeStruct((KEEP, 128), jnp.int32),
            jax.ShapeDtypeStruct((8, KEEP), jnp.int32),
            jax.ShapeDtypeStruct((8, 128), F32),
        ),
        in_specs=[SMEM] + [VMEM] * 3,
        out_specs=(VMEM,) * 5,
        scratch_shapes=[pltpu.VMEM((KEEP + MOVE, packed.shape[1]), BF16)],
        compiler_params=ROOM,
        cost_estimate=pl.CostEstimate(
            flops=100_000_000, bytes_accessed=2_000_000, transcendentals=0
        ),
    )(patch_counts, packed, coming, wide)


def by_parity(values):
    part = [values[:, 128 * i : 128 * (i + 1)] for i in range(6)]
    turned = [pltpu.roll(p, 64, 1) for p in part]
    low = lax.broadcasted_iota(jnp.int32, part[0].shape, 1) < 64
    even = [part[0], jnp.where(low, part[1], turned[3]), jnp.where(low, turned[3], turned[4])]
    odd = [jnp.where(low, turned[1], turned[2]), jnp.where(low, turned[2], part[4]), part[5]]
    return jnp.concatenate(even, axis=1), jnp.concatenate(odd, axis=1)


def norm_kernel(place_ref, *refs):
    blocks, (share_ref, own_ref, other_ref, chips_ref) = refs[:-4], refs[-4:]
    me, core = place_ref[0], place_ref[1]
    width = blocks[0].shape[1]
    values = [b[...].astype(F32) for b in blocks[:-2]]
    values.append(jnp.concatenate([blocks[-2][...], blocks[-1][...]], axis=0).astype(F32))
    offsets = [0]
    for step in range(1, N_MP // 2):
        offsets += [-step, step]
    offsets.append(N_MP // 2)
    features = width * N_MP
    mean = sum(jnp.sum(v, axis=1, keepdims=True) for v in values) / features
    spread = sum(jnp.sum((v - mean) * (v - mean), axis=1, keepdims=True) for v in values)
    scale = lax.rsqrt(spread / features + 1e-06)
    half = width // 2
    for offset, v in zip(offsets, values):
        place = lax.rem(me + offset + N_MP, N_MP)
        normed = (v - mean) * scale
        chips_ref[2 * place] = normed[:, :half].astype(BF16)
        chips_ref[2 * place + 1] = normed[:, half:].astype(BF16)
        even, odd = by_parity(normed)
        first = core == 0
        columns = pl.ds(pl.multiple_of(place * half, 128), half)
        own_ref[:, columns] = jnp.where(first, even, odd).astype(BF16)
        other_ref[:, columns] = jnp.where(first, odd, even).astype(BF16)
    start = pl.multiple_of(jnp.minimum(me, SHARES - 1) * SHARE, SHARE)
    share_ref[...] = chips_ref[:, pl.ds(start, SHARE), :]


def gather_norm(own, place):
    blocks = [own]
    ahead = back = own
    for _ in range(1, N_MP // 2):
        ahead = shift(ahead, "mp", N_MP, 1)
        back = shift(back, "mp", N_MP, -1)
        blocks += [ahead, back]
    half = own.shape[0] // 2
    blocks.append(shift(ahead[:half], "mp", N_MP, 1))
    blocks.append(shift(back[half:], "mp", N_MP, -1))
    rows, width = own.shape
    return pl.pallas_call(
        norm_kernel,
        out_shape=(
            jax.ShapeDtypeStruct((2 * N_MP, SHARE, width // 2), BF16),
            jax.ShapeDtypeStruct((rows, width * N_MP // 2), BF16),
            jax.ShapeDtypeStruct((rows, width * N_MP // 2), BF16),
        ),
        in_specs=[SMEM] + [VMEM] * len(blocks),
        out_specs=(VMEM, VMEM, VMEM),
        scratch_shapes=[pltpu.VMEM((2 * N_MP, rows, width // 2), BF16)],
        compiler_params=ROOM,
        cost_estimate=pl.CostEstimate(flops=4_000_000, bytes_accessed=4_000_000, transcendentals=0),
    )(place, *blocks)


def project_kernel(own_ref, other_ref, weight_ref, own_out, other_out):
    @pl.when(pl.program_id(0) == 0)
    def _():
        own_out[...] = jnp.zeros_like(own_out)
        other_out[...] = jnp.zeros_like(other_out)

    rows = own_ref.shape[0]
    chips, groups = weight_ref.shape[:2]
    left = jnp.concatenate([own_ref[...], other_ref[...]], axis=0)
    right = jnp.concatenate(
        [
            jnp.concatenate([weight_ref[i, group] for group in range(groups)], axis=1)
            for i in range(chips)
        ],
        axis=0,
    )
    product = jnp.dot(left, right, preferred_element_type=F32)
    own_out[...] += product[:rows]
    other_out[...] += product[rows:]


def project(own, other, weight):
    rows = own.shape[0]
    chips, groups, depth, span = weight.shape
    step = 4
    block = pl.BlockSpec((rows, step * depth), lambda i: (0, i))
    result = pl.BlockSpec((rows, groups * span), lambda i: (0, 0))
    return pl.pallas_call(
        project_kernel,
        grid=(chips // step,),
        out_shape=(jax.ShapeDtypeStruct((rows, groups * span), F32),) * 2,
        in_specs=[
            block,
            block,
            pl.BlockSpec((step, groups, depth, span), lambda i: (i, 0, 0, 0)),
        ],
        out_specs=(result, result),
        compiler_params=ROOM,
        cost_estimate=pl.CostEstimate(
            flops=1_360_000_000, bytes_accessed=9_000_000, transcendentals=0
        ),
    )(own, other, weight)


def dot_t(a, b):
    return lax.dot_general(a, b, (((1,), (1,)), ((), ())), preferred_element_type=F32)


def t_dot(a, b):
    return lax.dot_general(a, b, (((0,), (0,)), ((), ())), preferred_element_type=F32)


def norm_parts(values):
    center = values - jnp.mean(values, axis=-1, keepdims=True)
    scale = lax.rsqrt(jnp.mean(center * center, axis=-1, keepdims=True) + 1e-06)
    return center * scale, scale


def norm_grad(normed, scale, cotangent):
    along = jnp.mean(cotangent * normed, axis=-1, keepdims=True)
    return scale * (cotangent - jnp.mean(cotangent, axis=-1, keepdims=True) - normed * along)


def attend_kernel(raw_ref, more_ref, row_ref, column_ref, target_ref, total_ref, grad_ref):
    inverse_root = 1.0 / math.sqrt(HD)
    heads = target_ref.shape[1] // HD
    rows = raw_ref.shape[0]
    row_segment = row_ref[:, :1]
    valid = row_segment >= 0
    allowed = (row_segment == column_ref[:1, :]) & valid
    total = total_ref[:1, :1]
    squares = jnp.zeros((raw_ref.shape[0], HD), F32)
    for head in range(heads):
        cut = [slice((part * heads + head) * HD, (part * heads + head + 1) * HD) for part in range(3)]
        query, key, value = [raw_ref[:, c] + more_ref[:, c] for c in cut]
        query_exact, query_scale = norm_parts(query)
        key_exact, key_scale = norm_parts(key)
        query_normed = query_exact.astype(BF16)
        key_normed = key_exact.astype(BF16)
        value_rows = value.astype(BF16)
        scores = dot_t(query_normed, key_normed) * inverse_root
        exponent = jnp.where(allowed, jnp.exp(scores), 0.0)
        denominator = jnp.sum(exponent, axis=-1, keepdims=True)
        denominator = jnp.where(valid, denominator, 1.0)
        weights = (exponent / denominator).astype(BF16)
        attended = jnp.dot(weights, value_rows, preferred_element_type=F32)
        target = target_ref[:, head * HD : (head + 1) * HD].astype(F32)
        error = jnp.where(valid, attended - target, 0.0)
        squares += error * error
        out_grad = (error / total).astype(BF16)
        prob_grad = dot_t(out_grad, value_rows)
        grad_ref[:rows, cut[2]] = t_dot(weights, out_grad).astype(BF16)
        weight_float = weights.astype(F32)
        inner = jnp.sum(prob_grad * weight_float, axis=-1, keepdims=True)
        score_grad = (weight_float * (prob_grad - inner) * inverse_root).astype(BF16)
        query_cotangent = jnp.dot(score_grad, key_normed, preferred_element_type=F32)
        key_cotangent = t_dot(score_grad, query_normed)
        grad_ref[:rows, cut[0]] = norm_grad(query_exact, query_scale, query_cotangent).astype(BF16)
        grad_ref[:rows, cut[1]] = norm_grad(key_exact, key_scale, key_cotangent).astype(BF16)
    square = jnp.full((STATS, grad_ref.shape[1]), jnp.sum(squares), F32)
    high = square.astype(BF16).astype(F32)
    middle = (square - high).astype(BF16).astype(F32)
    low = square - high - middle
    place = lax.broadcasted_iota(jnp.int32, square.shape, 0)
    terms = jnp.where(place == 0, high, jnp.where(place == 1, middle, low))
    grad_ref[rows:, :] = jnp.where(place < 3, terms, 0.0).astype(BF16)


def attend(raw, more, column, row, targets, patch_total):
    rows, width = raw.shape
    return pl.pallas_call(
        attend_kernel,
        out_shape=jax.ShapeDtypeStruct((rows + STATS, width), BF16),
        in_specs=[VMEM] * 6,
        out_specs=VMEM,
        compiler_params=ROOM,
        cost_estimate=pl.CostEstimate(
            flops=50_000_000, bytes_accessed=1_500_000, transcendentals=30_000
        ),
    )(raw, more, column, row, targets, patch_total)


def turn_kernel(place_ref, blocks_ref, own_ref, other_ref):
    y, x, core = place_ref[0], place_ref[1], place_ref[2]
    half = blocks_ref.shape[3] // 2
    rows = SHARES * SHARE
    ring = (0, -1, 1, 2)
    pieces = []
    for far in ring:
        for near in ring:
            step_x = jnp.where(core == 0, near, far)
            step_y = jnp.where(core == 0, far, near)
            chip = lax.rem(y + step_y + SIDE, SIDE) * SIDE + lax.rem(x + step_x + SIDE, SIDE)
            pieces += [blocks_ref[share, chip] for share in range(SHARES)]
    for group in range(SIDE):
        several = pieces[group * SIDE * SHARES : (group + 1) * SIDE * SHARES]
        wide = jnp.concatenate(several, axis=0).astype(F32).T.astype(BF16)
        columns = slice(group * SIDE * rows, (group + 1) * SIDE * rows)
        first = core == 0
        own_ref[:, columns] = jnp.where(first, wide[:half], wide[half:])
        other_ref[:, columns] = jnp.where(first, wide[half:], wide[:half])


def turn_blocks(blocks, place):
    _, chips, _, feats = blocks.shape
    return pl.pallas_call(
        turn_kernel,
        out_shape=(jax.ShapeDtypeStruct((feats // 2, chips * KEEP), BF16),) * 2,
        in_specs=[SMEM, VMEM],
        out_specs=(VMEM, VMEM),
        compiler_params=ROOM,
        cost_estimate=pl.CostEstimate(flops=1_000_000, bytes_accessed=2_400_000, transcendentals=0),
    )(place, blocks)


def grad_kernel(parts, own_ref, other_ref, *refs):
    pieces, (own_out, other_out) = refs[:parts], refs[parts:]
    for left_ref, out_ref in ((other_ref, other_out), (own_ref, own_out)):
        groups, _, span = out_ref.shape
        total = None
        start = 0
        for piece in pieces:
            rows = piece.shape[0]
            product = jnp.dot(
                left_ref[:, start : start + rows], piece[...], preferred_element_type=F32
            )
            total = product if total is None else total + product
            start += rows
        for group in range(groups):
            out_ref[group] = total[:, group * span : (group + 1) * span]


def grad_first(own, other, pieces, groups):
    width = pieces[0].shape[1]
    part = jax.ShapeDtypeStruct((groups, own.shape[0], width // groups), F32)
    return pl.pallas_call(
        functools.partial(grad_kernel, len(pieces)),
        out_shape=(part, part),
        in_specs=[VMEM] * (2 + len(pieces)),
        out_specs=(VMEM, VMEM),
        compiler_params=ROOM,
        cost_estimate=pl.CostEstimate(
            flops=1_000_000_000, bytes_accessed=5_000_000, transcendentals=0
        ),
    )(own, other, *pieces)


def last_kernel(start, left_ref, piece_ref, part_ref, out_ref):
    rows = piece_ref.shape[0]
    product = jnp.dot(
        left_ref[:, start : start + rows], piece_ref[...], preferred_element_type=F32
    )
    groups, _, span = out_ref.shape
    for group in range(groups):
        out_ref[group] = part_ref[group] + product[:, group * span : (group + 1) * span]


def grad_last(left, piece, part):
    return pl.pallas_call(
        functools.partial(last_kernel, left.shape[1] - piece.shape[0]),
        out_shape=jax.ShapeDtypeStruct(part.shape, F32),
        in_specs=[VMEM] * 3,
        out_specs=VMEM,
        compiler_params=ROOM,
        cost_estimate=pl.CostEstimate(
            flops=170_000_000, bytes_accessed=3_000_000, transcendentals=0
        ),
    )(left, piece, part)


def finish_kernel(a_ref, b_ref, sum_ref, more_ref, total_ref, out_ref, loss_ref):
    out_ref[...] = a_ref[...] + b_ref[...]
    squared = sum_ref[:1, :1] + more_ref[:1, :1]
    loss_ref[...] = squared / (2.0 * total_ref[:1, :1])


def finish(a, b, squared, more, total):
    return pl.pallas_call(
        finish_kernel,
        out_shape=(jax.ShapeDtypeStruct(a.shape, F32), jax.ShapeDtypeStruct((1, 1), F32)),
        in_specs=[VMEM] * 5,
        out_specs=(VMEM, VMEM),
        compiler_params=ROOM,
        cost_estimate=pl.CostEstimate(flops=300_000, bytes_accessed=2_700_000, transcendentals=0),
    )(a, b, squared, more, total)


def near_kernel(*refs):
    blocks, (out_ref, sum_ref) = refs[:-2], refs[-2:]
    rows = blocks[0].shape[0] - STATS
    terms = 0.0
    for index, block in enumerate(blocks):
        out_ref[index * rows : (index + 1) * rows, :] = block[:rows, :]
        terms += block[rows:, :128].astype(F32)
    sum_ref[...] = jnp.broadcast_to(jnp.sum(terms, axis=0, keepdims=True), sum_ref.shape)


def near_rows(blocks):
    rows, width = blocks[0].shape
    return pl.pallas_call(
        near_kernel,
        out_shape=(
            jax.ShapeDtypeStruct((len(blocks) * (rows - STATS), width), BF16),
            jax.ShapeDtypeStruct((8, 128), F32),
        ),
        in_specs=[VMEM] * len(blocks),
        out_specs=(VMEM, VMEM),
        compiler_params=ROOM,
        cost_estimate=pl.CostEstimate(flops=100_000, bytes_accessed=1_800_000, transcendentals=0),
    )(*blocks)


def local(patches, embed_weight, project_weight, patch_counts, segment_ids, targets):
    whole_weight = lax.all_gather(project_weight.transpose(1, 0, 2), ("y", "x"), axis=0)
    y, x, core, mp = [lax.axis_index(a) for a in ("y", "x", "core", "mp")]

    packed, leaving, embed_part = pack(patches, targets, segment_ids, patch_counts, embed_weight)
    half = CHIPS * CORES // 2
    coming = lax.ppermute(leaving, DP, [(i + half, i) for i in range(half)])
    wide = lax.all_gather(embed_part, DP, axis=0, tiled=True)
    own_features, targets, column, row, total_tile = embed(patch_counts, packed, coming, wide)
    chip_blocks, own_half, other_half = gather_norm(own_features, jnp.stack([mp, core]))
    chip_share = lax.all_to_all(chip_blocks, ("y", "x"), split_axis=0, concat_axis=0, tiled=True)
    more_half, chip_share = lax.optimization_barrier((swap(other_half), chip_share))
    chip_rows = lax.all_gather(chip_share, "mp", axis=0)
    own_part, other_part = project(own_half, more_half, whole_weight)
    grad_rows = attend(own_part, swap(other_part), column, row, targets, total_tile)

    near, tile = near_rows(
        lax.optimization_barrier(
            (
                grad_rows,
                turn(grad_rows, True, 1),
                turn(grad_rows, True, -1),
                turn(grad_rows, True, 2),
            )
        )
    )
    behind, ahead = turn(near, False, 1), turn(near, False, -1)
    tile = tile + shift(tile, "mp", N_MP, 1)
    tile = tile + turn(tile, False, -1)
    behind, ahead, tile = lax.optimization_barrier((behind, ahead, tile))
    opposite = turn(behind, False, 1)
    for step in (2, 4):
        tile = tile + shift(tile, "mp", N_MP, step)
    tile = tile + turn(tile, False, -2)
    own_left, other_left = turn_blocks(chip_rows, jnp.stack([y, x, core]))
    groups = project_weight.shape[1]
    own_grad, other_grad = grad_first(own_left, other_left, (near, behind, ahead), groups)
    opposite, tile, own_grad, other_grad = lax.optimization_barrier(
        (opposite, tile, own_grad, other_grad)
    )
    more_grad, more_tile = lax.optimization_barrier(
        (swap(grad_last(other_left, opposite, other_grad)), swap(tile))
    )
    weight_grad, loss_tile = finish(
        grad_last(own_left, opposite, own_grad), more_grad, tile, more_tile, total_tile
    )
    loss_value = loss_tile[0, 0]
    return (weight_grad.transpose(1, 0, 2), loss_value)


def solution(mesh):
    chips = Mesh(mesh.devices.reshape(SIDE, SIDE, CORES, N_MP), DP + ("mp",))
    in_specs = (
        P(DP, None),
        P(("mp",) + DP, None),
        P(DP, None, "mp"),
        P(DP),
        P(DP),
        P(DP, "mp"),
    )
    out_specs = (P(DP, None, "mp"), P())
    return jax.shard_map(
        local, mesh=chips, in_specs=in_specs, out_specs=out_specs, check_vma=False
    )
```

```python
import functools
import math

import jax
import jax.numpy as jnp
from jax import lax
from jax.experimental import pallas as pl
from jax.experimental.pallas import tpu as pltpu
from jax.sharding import Mesh
from jax.sharding import PartitionSpec as P

HD = 128
KEEP = 96
MOVE = 64
P_SIZE = 588
PAD_P = 640
SHARE = 16
SHARES = KEEP // SHARE
STATS = 16
SEGMENT = 600
SIDE = 4
CHIPS = 16
CORES = 2
N_MP = 8
DP = ("y", "x", "core")
F32 = jnp.float32
BF16 = jnp.bfloat16
VMEM = pl.BlockSpec(memory_space=pltpu.VMEM)
SMEM = pl.BlockSpec(memory_space=pltpu.SMEM)
ROOM = pltpu.CompilerParams(vmem_limit_bytes=48 * 1024 * 1024)


def shift(array, axis, size, step):
    return lax.ppermute(array, axis, [(i, (i + step) % size) for i in range(size)])


def swap(array):
    return lax.ppermute(array, "core", [(0, 1), (1, 0)])


def turn(array, first, step):
    pairs = []
    for y in range(SIDE):
        for x in range(SIDE):
            for core in range(CORES):
                along_x = (core == 0) == first
                to_y = y if along_x else (y + step) % SIDE
                to_x = (x + step) % SIDE if along_x else x
                pairs.append(((y * SIDE + x) * CORES + core, (to_y * SIDE + to_x) * CORES + core))
    return lax.ppermute(array, DP, pairs)


def rows_kept(counts_ref):
    end = jnp.int32(0)
    kept = jnp.int32(0)
    for slot in range(counts_ref.shape[0]):
        end = end + counts_ref[slot]
        kept = jnp.where(end <= KEEP, end, kept)
    return pl.multiple_of(kept, 16), end


def pack_kernel(counts_ref, *refs):
    sources, (all_ref, leave_ref, wide_ref, tall), rest = refs[:4], refs[4:8], refs[8:]
    places, sem = rest[:4], rest[4]
    copies = [
        pltpu.make_async_copy(source, place, sem.at[index])
        for index, (source, place) in enumerate(zip(sources, places))
    ]
    for copy in copies:
        copy.start()
    for copy in copies:
        copy.wait()
    patch_ref, target_ref, segment_ref, embed_ref = places
    p_size, rows = patch_ref.shape
    tall[...] = jnp.zeros_like(tall)
    tall[:p_size, :] = patch_ref[...].astype(F32)
    marks = jnp.broadcast_to(segment_ref[...].astype(F32) + 1.0, (8, rows))
    tall[SEGMENT : SEGMENT + 8, :] = marks
    all_ref[:rows, :PAD_P] = tall[...].T.astype(BF16)
    all_ref[:rows, PAD_P:] = target_ref[...]
    all_ref[rows:, :] = jnp.zeros((all_ref.shape[0] - rows, all_ref.shape[1]), BF16)
    kept, total = rows_kept(counts_ref)
    leave_ref[...] = all_ref[pl.ds(kept, MOVE), :]
    row = lax.broadcasted_iota(jnp.int32, (wide_ref.shape[0], wide_ref.shape[1] - 512), 0)
    column = lax.broadcasted_iota(jnp.int32, (wide_ref.shape[0], wide_ref.shape[1] - 512), 1)
    here = (row == 0) & (column == p_size - 512)
    wide_ref[:, 512:] = jnp.where(here, total.astype(F32), 0.0).astype(BF16)
    wide_ref[:, :p_size] = embed_ref[...]


def pack(patches, targets, segment_ids, patch_counts, embed_weight):
    rows, p_size = patches.shape
    width = PAD_P + targets.shape[1]
    return pl.pallas_call(
        pack_kernel,
        out_shape=(
            jax.ShapeDtypeStruct((rows + MOVE, width), BF16),
            jax.ShapeDtypeStruct((MOVE, width), BF16),
            jax.ShapeDtypeStruct((embed_weight.shape[0], PAD_P), BF16),
        ),
        in_specs=[SMEM] + [pl.BlockSpec(memory_space=pltpu.HBM)] * 4,
        out_specs=(VMEM, VMEM, VMEM),
        scratch_shapes=[
            pltpu.VMEM((PAD_P, rows), F32),
            pltpu.VMEM((p_size, rows), BF16),
            pltpu.VMEM(targets.shape, BF16),
            pltpu.VMEM((1, rows), jnp.int32),
            pltpu.VMEM(embed_weight.shape, BF16),
            pltpu.SemaphoreType.DMA((4,)),
        ],
        cost_estimate=pl.CostEstimate(flops=1_000_000, bytes_accessed=1_000_000, transcendentals=0),
    )(patch_counts, patches.T, targets, segment_ids.reshape(1, rows), embed_weight)


def embed_kernel(counts_ref, all_ref, come_ref, wide_ref, out_ref, target_ref, column_ref, row_ref, total_ref, around):
    kept, _ = rows_kept(counts_ref)
    around[...] = jnp.zeros_like(around)
    around[pl.ds(kept, MOVE), :] = come_ref[...]
    mine = lax.broadcasted_iota(jnp.int32, (KEEP, 1), 0) < kept
    merged = jnp.where(mine, all_ref[:KEEP, :], around[:KEEP, :])
    target_ref[...] = merged[:, PAD_P:]
    marks = merged[:, PAD_P - 128 : PAD_P].astype(F32)
    slot = lax.broadcasted_iota(jnp.int32, marks.shape, 1) == SEGMENT - (PAD_P - 128)
    mark = jnp.sum(jnp.where(slot, marks, 0.0), axis=1, keepdims=True) - 1.0
    spread = jnp.broadcast_to(mark, marks.shape)
    column_ref[...] = spread.astype(jnp.int32)
    row_ref[...] = spread.T[:8, :].astype(jnp.int32)
    tail = wide_ref[:, PAD_P - 128 : PAD_P].astype(F32)
    slot = lax.broadcasted_iota(jnp.int32, tail.shape, 1) == P_SIZE - (PAD_P - 128)
    total_ref[...] = jnp.full(total_ref.shape, jnp.sum(jnp.where(slot, tail, 0.0)), F32)
    out_ref[...] = dot_t(merged[:, :PAD_P], wide_ref[...]).astype(BF16)


def embed(patch_counts, packed, coming, wide):
    targets = packed.shape[1] - PAD_P
    return pl.pallas_call(
        embed_kernel,
        out_shape=(
            jax.ShapeDtypeStruct((KEEP, wide.shape[0]), BF16),
            jax.ShapeDtypeStruct((KEEP, targets), BF16),
            jax.ShapeDtypeStruct((KEEP, 128), jnp.int32),
            jax.ShapeDtypeStruct((8, KEEP), jnp.int32),
            jax.ShapeDtypeStruct((8, 128), F32),
        ),
        in_specs=[SMEM] + [VMEM] * 3,
        out_specs=(VMEM,) * 5,
        scratch_shapes=[pltpu.VMEM((KEEP + MOVE, packed.shape[1]), BF16)],
        compiler_params=ROOM,
        cost_estimate=pl.CostEstimate(
            flops=100_000_000, bytes_accessed=2_000_000, transcendentals=0
        ),
    )(patch_counts, packed, coming, wide)


def by_parity(values):
    part = [values[:, 128 * i : 128 * (i + 1)] for i in range(6)]
    turned = [pltpu.roll(p, 64, 1) for p in part]
    low = lax.broadcasted_iota(jnp.int32, part[0].shape, 1) < 64
    even = [part[0], jnp.where(low, part[1], turned[3]), jnp.where(low, turned[3], turned[4])]
    odd = [jnp.where(low, turned[1], turned[2]), jnp.where(low, turned[2], part[4]), part[5]]
    return jnp.concatenate(even, axis=1), jnp.concatenate(odd, axis=1)


def norm_kernel(place_ref, *refs):
    blocks, (share_ref, own_ref, other_ref, chips_ref) = refs[:-4], refs[-4:]
    me, core = place_ref[0], place_ref[1]
    width = blocks[0].shape[1]
    values = [b[...].astype(F32) for b in blocks[:-2]]
    values.append(jnp.concatenate([blocks[-2][...], blocks[-1][...]], axis=0).astype(F32))
    offsets = [0]
    for step in range(1, N_MP // 2):
        offsets += [-step, step]
    offsets.append(N_MP // 2)
    features = width * N_MP
    mean = sum(jnp.sum(v, axis=1, keepdims=True) for v in values) / features
    spread = sum(jnp.sum((v - mean) * (v - mean), axis=1, keepdims=True) for v in values)
    scale = lax.rsqrt(spread / features + 1e-06)
    half = width // 2
    for offset, v in zip(offsets, values):
        place = lax.rem(me + offset + N_MP, N_MP)
        normed = (v - mean) * scale
        chips_ref[2 * place] = normed[:, :half].astype(BF16)
        chips_ref[2 * place + 1] = normed[:, half:].astype(BF16)
        even, odd = by_parity(normed)
        first = core == 0
        columns = pl.ds(pl.multiple_of(place * half, 128), half)
        own_ref[:, columns] = jnp.where(first, even, odd).astype(BF16)
        other_ref[:, columns] = jnp.where(first, odd, even).astype(BF16)
    start = pl.multiple_of(jnp.minimum(me, SHARES - 1) * SHARE, SHARE)
    share_ref[...] = chips_ref[:, pl.ds(start, SHARE), :]


def gather_norm(own, place):
    blocks = [own]
    ahead = back = own
    for _ in range(1, N_MP // 2):
        ahead = shift(ahead, "mp", N_MP, 1)
        back = shift(back, "mp", N_MP, -1)
        blocks += [ahead, back]
    half = own.shape[0] // 2
    blocks.append(shift(ahead[:half], "mp", N_MP, 1))
    blocks.append(shift(back[half:], "mp", N_MP, -1))
    rows, width = own.shape
    return pl.pallas_call(
        norm_kernel,
        out_shape=(
            jax.ShapeDtypeStruct((2 * N_MP, SHARE, width // 2), BF16),
            jax.ShapeDtypeStruct((rows, width * N_MP // 2), BF16),
            jax.ShapeDtypeStruct((rows, width * N_MP // 2), BF16),
        ),
        in_specs=[SMEM] + [VMEM] * len(blocks),
        out_specs=(VMEM, VMEM, VMEM),
        scratch_shapes=[pltpu.VMEM((2 * N_MP, rows, width // 2), BF16)],
        compiler_params=ROOM,
        cost_estimate=pl.CostEstimate(flops=4_000_000, bytes_accessed=4_000_000, transcendentals=0),
    )(place, *blocks)


def project_kernel(own_ref, other_ref, weight_ref, own_out, other_out):
    @pl.when(pl.program_id(0) == 0)
    def _():
        own_out[...] = jnp.zeros_like(own_out)
        other_out[...] = jnp.zeros_like(other_out)

    rows = own_ref.shape[0]
    chips, groups = weight_ref.shape[:2]
    left = jnp.concatenate([own_ref[...], other_ref[...]], axis=0)
    right = jnp.concatenate(
        [
            jnp.concatenate([weight_ref[i, group] for group in range(groups)], axis=1)
            for i in range(chips)
        ],
        axis=0,
    )
    product = jnp.dot(left, right, preferred_element_type=F32)
    own_out[...] += product[:rows]
    other_out[...] += product[rows:]


def project(own, other, weight):
    rows = own.shape[0]
    chips, groups, depth, span = weight.shape
    step = 4
    block = pl.BlockSpec((rows, step * depth), lambda i: (0, i))
    result = pl.BlockSpec((rows, groups * span), lambda i: (0, 0))
    return pl.pallas_call(
        project_kernel,
        grid=(chips // step,),
        out_shape=(jax.ShapeDtypeStruct((rows, groups * span), F32),) * 2,
        in_specs=[
            block,
            block,
            pl.BlockSpec((step, groups, depth, span), lambda i: (i, 0, 0, 0)),
        ],
        out_specs=(result, result),
        compiler_params=ROOM,
        cost_estimate=pl.CostEstimate(
            flops=1_360_000_000, bytes_accessed=9_000_000, transcendentals=0
        ),
    )(own, other, weight)


def dot_t(a, b):
    return lax.dot_general(a, b, (((1,), (1,)), ((), ())), preferred_element_type=F32)


def t_dot(a, b):
    return lax.dot_general(a, b, (((0,), (0,)), ((), ())), preferred_element_type=F32)


def norm_parts(values):
    center = values - jnp.mean(values, axis=-1, keepdims=True)
    scale = lax.rsqrt(jnp.mean(center * center, axis=-1, keepdims=True) + 1e-06)
    return center * scale, scale


def norm_grad(normed, scale, cotangent):
    along = jnp.mean(cotangent * normed, axis=-1, keepdims=True)
    return scale * (cotangent - jnp.mean(cotangent, axis=-1, keepdims=True) - normed * along)


def attend_kernel(raw_ref, more_ref, row_ref, column_ref, target_ref, total_ref, grad_ref):
    inverse_root = 1.0 / math.sqrt(HD)
    heads = target_ref.shape[1] // HD
    rows = raw_ref.shape[0]
    row_segment = row_ref[:, :1]
    valid = row_segment >= 0
    allowed = (row_segment == column_ref[:1, :]) & valid
    total = total_ref[:1, :1]
    squares = jnp.zeros((raw_ref.shape[0], HD), F32)
    for head in range(heads):
        cut = [slice((part * heads + head) * HD, (part * heads + head + 1) * HD) for part in range(3)]
        query, key, value = [raw_ref[:, c] + more_ref[:, c] for c in cut]
        query_exact, query_scale = norm_parts(query)
        key_exact, key_scale = norm_parts(key)
        query_normed = query_exact.astype(BF16)
        key_normed = key_exact.astype(BF16)
        value_rows = value.astype(BF16)
        scores = dot_t(query_normed, key_normed) * inverse_root
        exponent = jnp.where(allowed, jnp.exp(scores), 0.0)
        denominator = jnp.sum(exponent, axis=-1, keepdims=True)
        denominator = jnp.where(valid, denominator, 1.0)
        weights = (exponent / denominator).astype(BF16)
        attended = jnp.dot(weights, value_rows, preferred_element_type=F32)
        target = target_ref[:, head * HD : (head + 1) * HD].astype(F32)
        error = jnp.where(valid, attended - target, 0.0)
        squares += error * error
        out_grad = (error / total).astype(BF16)
        prob_grad = dot_t(out_grad, value_rows)
        grad_ref[:rows, cut[2]] = t_dot(weights, out_grad).astype(BF16)
        weight_float = weights.astype(F32)
        inner = jnp.sum(prob_grad * weight_float, axis=-1, keepdims=True)
        score_grad = (weight_float * (prob_grad - inner) * inverse_root).astype(BF16)
        query_cotangent = jnp.dot(score_grad, key_normed, preferred_element_type=F32)
        key_cotangent = t_dot(score_grad, query_normed)
        grad_ref[:rows, cut[0]] = norm_grad(query_exact, query_scale, query_cotangent).astype(BF16)
        grad_ref[:rows, cut[1]] = norm_grad(key_exact, key_scale, key_cotangent).astype(BF16)
    square = jnp.full((STATS, grad_ref.shape[1]), jnp.sum(squares), F32)
    high = square.astype(BF16).astype(F32)
    middle = (square - high).astype(BF16).astype(F32)
    low = square - high - middle
    place = lax.broadcasted_iota(jnp.int32, square.shape, 0)
    terms = jnp.where(place == 0, high, jnp.where(place == 1, middle, low))
    grad_ref[rows:, :] = jnp.where(place < 3, terms, 0.0).astype(BF16)


def attend(raw, more, column, row, targets, patch_total):
    rows, width = raw.shape
    return pl.pallas_call(
        attend_kernel,
        out_shape=jax.ShapeDtypeStruct((rows + STATS, width), BF16),
        in_specs=[VMEM] * 6,
        out_specs=VMEM,
        compiler_params=ROOM,
        cost_estimate=pl.CostEstimate(
            flops=50_000_000, bytes_accessed=1_500_000, transcendentals=30_000
        ),
    )(raw, more, column, row, targets, patch_total)


def turn_kernel(place_ref, blocks_ref, own_ref, other_ref):
    y, x, core = place_ref[0], place_ref[1], place_ref[2]
    half = blocks_ref.shape[3] // 2
    rows = SHARES * SHARE
    ring = (0, -1, 1, 2)
    pieces = []
    for far in ring:
        for near in ring:
            step_x = jnp.where(core == 0, near, far)
            step_y = jnp.where(core == 0, far, near)
            chip = lax.rem(y + step_y + SIDE, SIDE) * SIDE + lax.rem(x + step_x + SIDE, SIDE)
            pieces += [blocks_ref[share, chip] for share in range(SHARES)]
    for group in range(SIDE):
        several = pieces[group * SIDE * SHARES : (group + 1) * SIDE * SHARES]
        wide = jnp.concatenate(several, axis=0).astype(F32).T.astype(BF16)
        columns = slice(group * SIDE * rows, (group + 1) * SIDE * rows)
        first = core == 0
        own_ref[:, columns] = jnp.where(first, wide[:half], wide[half:])
        other_ref[:, columns] = jnp.where(first, wide[half:], wide[:half])


def turn_blocks(blocks, place):
    _, chips, _, feats = blocks.shape
    return pl.pallas_call(
        turn_kernel,
        out_shape=(jax.ShapeDtypeStruct((feats // 2, chips * KEEP), BF16),) * 2,
        in_specs=[SMEM, VMEM],
        out_specs=(VMEM, VMEM),
        compiler_params=ROOM,
        cost_estimate=pl.CostEstimate(flops=1_000_000, bytes_accessed=2_400_000, transcendentals=0),
    )(place, blocks)


def grad_kernel(parts, own_ref, other_ref, *refs):
    pieces, (own_out, other_out) = refs[:parts], refs[parts:]
    for left_ref, out_ref in ((other_ref, other_out), (own_ref, own_out)):
        groups, _, span = out_ref.shape
        total = None
        start = 0
        for piece in pieces:
            rows = piece.shape[0]
            product = jnp.dot(
                left_ref[:, start : start + rows], piece[...], preferred_element_type=F32
            )
            total = product if total is None else total + product
            start += rows
        for group in range(groups):
            out_ref[group] = total[:, group * span : (group + 1) * span]


def grad_first(own, other, pieces, groups):
    width = pieces[0].shape[1]
    part = jax.ShapeDtypeStruct((groups, own.shape[0], width // groups), F32)
    return pl.pallas_call(
        functools.partial(grad_kernel, len(pieces)),
        out_shape=(part, part),
        in_specs=[VMEM] * (2 + len(pieces)),
        out_specs=(VMEM, VMEM),
        compiler_params=ROOM,
        cost_estimate=pl.CostEstimate(
            flops=1_000_000_000, bytes_accessed=5_000_000, transcendentals=0
        ),
    )(own, other, *pieces)


def last_kernel(start, left_ref, piece_ref, part_ref, out_ref):
    rows = piece_ref.shape[0]
    product = jnp.dot(
        left_ref[:, start : start + rows], piece_ref[...], preferred_element_type=F32
    )
    groups, _, span = out_ref.shape
    for group in range(groups):
        out_ref[group] = part_ref[group] + product[:, group * span : (group + 1) * span]


def grad_last(left, piece, part):
    return pl.pallas_call(
        functools.partial(last_kernel, left.shape[1] - piece.shape[0]),
        out_shape=jax.ShapeDtypeStruct(part.shape, F32),
        in_specs=[VMEM] * 3,
        out_specs=VMEM,
        compiler_params=ROOM,
        cost_estimate=pl.CostEstimate(
            flops=170_000_000, bytes_accessed=3_000_000, transcendentals=0
        ),
    )(left, piece, part)


def finish_kernel(a_ref, b_ref, sum_ref, more_ref, total_ref, out_ref, loss_ref):
    out_ref[...] = a_ref[...] + b_ref[...]
    squared = sum_ref[:1, :1] + more_ref[:1, :1]
    loss_ref[...] = squared / (2.0 * total_ref[:1, :1])


def finish(a, b, squared, more, total):
    return pl.pallas_call(
        finish_kernel,
        out_shape=(jax.ShapeDtypeStruct(a.shape, F32), jax.ShapeDtypeStruct((1, 1), F32)),
        in_specs=[VMEM] * 5,
        out_specs=(VMEM, VMEM),
        compiler_params=ROOM,
        cost_estimate=pl.CostEstimate(flops=300_000, bytes_accessed=2_700_000, transcendentals=0),
    )(a, b, squared, more, total)


def near_kernel(*refs):
    blocks, (out_ref, sum_ref) = refs[:-2], refs[-2:]
    rows = blocks[0].shape[0] - STATS
    terms = 0.0
    for index, block in enumerate(blocks):
        out_ref[index * rows : (index + 1) * rows, :] = block[:rows, :]
        terms += block[rows:, :128].astype(F32)
    sum_ref[...] = jnp.broadcast_to(jnp.sum(terms, axis=0, keepdims=True), sum_ref.shape)


def near_rows(blocks):
    rows, width = blocks[0].shape
    return pl.pallas_call(
        near_kernel,
        out_shape=(
            jax.ShapeDtypeStruct((len(blocks) * (rows - STATS), width), BF16),
            jax.ShapeDtypeStruct((8, 128), F32),
        ),
        in_specs=[VMEM] * len(blocks),
        out_specs=(VMEM, VMEM),
        compiler_params=ROOM,
        cost_estimate=pl.CostEstimate(flops=100_000, bytes_accessed=1_800_000, transcendentals=0),
    )(*blocks)


def local(patches, embed_weight, project_weight, patch_counts, segment_ids, targets):
    whole_weight = lax.all_gather(project_weight.transpose(1, 0, 2), ("y", "x"), axis=0)
    y, x, core, mp = [lax.axis_index(a) for a in ("y", "x", "core", "mp")]

    packed, leaving, embed_part = pack(patches, targets, segment_ids, patch_counts, embed_weight)
    half = CHIPS * CORES // 2
    coming = lax.ppermute(leaving, DP, [(i + half, i) for i in range(half)])
    wide = lax.all_gather(embed_part, DP, axis=0, tiled=True)
    own_features, targets, column, row, total_tile = embed(patch_counts, packed, coming, wide)
    chip_blocks, own_half, other_half = gather_norm(own_features, jnp.stack([mp, core]))
    chip_share = lax.all_to_all(chip_blocks, ("y", "x"), split_axis=0, concat_axis=0, tiled=True)
    more_half, chip_share = lax.optimization_barrier((swap(other_half), chip_share))
    chip_rows = lax.all_gather(chip_share, "mp", axis=0)
    own_part, other_part = project(own_half, more_half, whole_weight)
    grad_rows = attend(own_part, swap(other_part), column, row, targets, total_tile)

    near, tile = near_rows(
        lax.optimization_barrier(
            (
                grad_rows,
                turn(grad_rows, True, 1),
                turn(grad_rows, True, -1),
                turn(grad_rows, True, 2),
            )
        )
    )
    behind, ahead = turn(near, False, 1), turn(near, False, -1)
    tile = sum((shift(tile, "mp", N_MP, step) for step in (1, 2, 3)), tile)
    tile = tile + turn(tile, False, -1)
    behind, ahead, tile = lax.optimization_barrier((behind, ahead, tile))
    opposite = turn(behind, False, 1)
    tile = tile + shift(tile, "mp", N_MP, 4)
    tile = tile + turn(tile, False, -2)
    own_left, other_left = turn_blocks(chip_rows, jnp.stack([y, x, core]))
    groups = project_weight.shape[1]
    own_grad, other_grad = grad_first(own_left, other_left, (near, behind, ahead), groups)
    opposite, tile, own_grad, other_grad = lax.optimization_barrier(
        (opposite, tile, own_grad, other_grad)
    )
    more_grad, more_tile = lax.optimization_barrier(
        (swap(grad_last(other_left, opposite, other_grad)), swap(tile))
    )
    weight_grad, loss_tile = finish(
        grad_last(own_left, opposite, own_grad), more_grad, tile, more_tile, total_tile
    )
    loss_value = loss_tile[0, 0]
    return (weight_grad.transpose(1, 0, 2), loss_value)


def solution(mesh):
    chips = Mesh(mesh.devices.reshape(SIDE, SIDE, CORES, N_MP), DP + ("mp",))
    in_specs = (
        P(DP, None),
        P(("mp",) + DP, None),
        P(DP, None, "mp"),
        P(DP),
        P(DP),
        P(DP, "mp"),
    )
    out_specs = (P(DP, None, "mp"), P())
    return jax.shard_map(
        local, mesh=chips, in_specs=in_specs, out_specs=out_specs, check_vma=False
    )
```

```python
import functools
import math

import jax
import jax.numpy as jnp
from jax import lax
from jax.experimental import pallas as pl
from jax.experimental.pallas import tpu as pltpu
from jax.sharding import Mesh
from jax.sharding import PartitionSpec as P

HD = 128
KEEP = 96
MOVE = 64
P_SIZE = 588
PAD_P = 640
SHARE = 16
SHARES = KEEP // SHARE
STATS = 16
SEGMENT = 600
SIDE = 4
CHIPS = 16
CORES = 2
N_MP = 8
DP = ("y", "x", "core")
F32 = jnp.float32
BF16 = jnp.bfloat16
VMEM = pl.BlockSpec(memory_space=pltpu.VMEM)
SMEM = pl.BlockSpec(memory_space=pltpu.SMEM)
ROOM = pltpu.CompilerParams(vmem_limit_bytes=48 * 1024 * 1024)


def shift(array, axis, size, step):
    return lax.ppermute(array, axis, [(i, (i + step) % size) for i in range(size)])


def swap(array):
    return lax.ppermute(array, "core", [(0, 1), (1, 0)])


def turn(array, first, step):
    pairs = []
    for y in range(SIDE):
        for x in range(SIDE):
            for core in range(CORES):
                along_x = (core == 0) == first
                to_y = y if along_x else (y + step) % SIDE
                to_x = (x + step) % SIDE if along_x else x
                pairs.append(((y * SIDE + x) * CORES + core, (to_y * SIDE + to_x) * CORES + core))
    return lax.ppermute(array, DP, pairs)


def rows_kept(counts_ref):
    end = jnp.int32(0)
    kept = jnp.int32(0)
    for slot in range(counts_ref.shape[0]):
        end = end + counts_ref[slot]
        kept = jnp.where(end <= KEEP, end, kept)
    return pl.multiple_of(kept, 16), end


def pack_kernel(counts_ref, *refs):
    sources, (all_ref, leave_ref, wide_ref, tall), rest = refs[:4], refs[4:8], refs[8:]
    places, sem = rest[:4], rest[4]
    copies = [
        pltpu.make_async_copy(source, place, sem.at[index])
        for index, (source, place) in enumerate(zip(sources, places))
    ]
    for copy in copies:
        copy.start()
    for copy in copies:
        copy.wait()
    patch_ref, target_ref, segment_ref, embed_ref = places
    p_size, rows = patch_ref.shape
    tall[...] = jnp.zeros_like(tall)
    tall[:p_size, :] = patch_ref[...].astype(F32)
    marks = jnp.broadcast_to(segment_ref[...].astype(F32) + 1.0, (8, rows))
    tall[SEGMENT : SEGMENT + 8, :] = marks
    all_ref[:rows, :PAD_P] = tall[...].T.astype(BF16)
    all_ref[:rows, PAD_P:] = target_ref[...]
    all_ref[rows:, :] = jnp.zeros((all_ref.shape[0] - rows, all_ref.shape[1]), BF16)
    kept, total = rows_kept(counts_ref)
    leave_ref[...] = all_ref[pl.ds(kept, MOVE), :]
    row = lax.broadcasted_iota(jnp.int32, (wide_ref.shape[0], wide_ref.shape[1] - 512), 0)
    column = lax.broadcasted_iota(jnp.int32, (wide_ref.shape[0], wide_ref.shape[1] - 512), 1)
    here = (row == 0) & (column == p_size - 512)
    wide_ref[:, 512:] = jnp.where(here, total.astype(F32), 0.0).astype(BF16)
    wide_ref[:, :p_size] = embed_ref[...]


def pack(patches, targets, segment_ids, patch_counts, embed_weight):
    rows, p_size = patches.shape
    width = PAD_P + targets.shape[1]
    return pl.pallas_call(
        pack_kernel,
        out_shape=(
            jax.ShapeDtypeStruct((rows + MOVE, width), BF16),
            jax.ShapeDtypeStruct((MOVE, width), BF16),
            jax.ShapeDtypeStruct((embed_weight.shape[0], PAD_P), BF16),
        ),
        in_specs=[SMEM] + [pl.BlockSpec(memory_space=pltpu.HBM)] * 4,
        out_specs=(VMEM, VMEM, VMEM),
        scratch_shapes=[
            pltpu.VMEM((PAD_P, rows), F32),
            pltpu.VMEM((p_size, rows), BF16),
            pltpu.VMEM(targets.shape, BF16),
            pltpu.VMEM((1, rows), jnp.int32),
            pltpu.VMEM(embed_weight.shape, BF16),
            pltpu.SemaphoreType.DMA((4,)),
        ],
        cost_estimate=pl.CostEstimate(flops=1_000_000, bytes_accessed=1_000_000, transcendentals=0),
    )(patch_counts, patches.T, targets, segment_ids.reshape(1, rows), embed_weight)


def embed_kernel(counts_ref, all_ref, come_ref, wide_ref, out_ref, target_ref, column_ref, row_ref, total_ref, around):
    kept, _ = rows_kept(counts_ref)
    around[...] = jnp.zeros_like(around)
    around[pl.ds(kept, MOVE), :] = come_ref[...]
    mine = lax.broadcasted_iota(jnp.int32, (KEEP, 1), 0) < kept
    merged = jnp.where(mine, all_ref[:KEEP, :], around[:KEEP, :])
    target_ref[...] = merged[:, PAD_P:]
    marks = merged[:, PAD_P - 128 : PAD_P].astype(F32)
    slot = lax.broadcasted_iota(jnp.int32, marks.shape, 1) == SEGMENT - (PAD_P - 128)
    mark = jnp.sum(jnp.where(slot, marks, 0.0), axis=1, keepdims=True) - 1.0
    spread = jnp.broadcast_to(mark, marks.shape)
    column_ref[...] = spread.astype(jnp.int32)
    row_ref[...] = spread.T[:8, :].astype(jnp.int32)
    tail = wide_ref[:, PAD_P - 128 : PAD_P].astype(F32)
    slot = lax.broadcasted_iota(jnp.int32, tail.shape, 1) == P_SIZE - (PAD_P - 128)
    total_ref[...] = jnp.full(total_ref.shape, jnp.sum(jnp.where(slot, tail, 0.0)), F32)
    out_ref[...] = dot_t(merged[:, :PAD_P], wide_ref[...]).astype(BF16)


def embed(patch_counts, packed, coming, wide):
    targets = packed.shape[1] - PAD_P
    return pl.pallas_call(
        embed_kernel,
        out_shape=(
            jax.ShapeDtypeStruct((KEEP, wide.shape[0]), BF16),
            jax.ShapeDtypeStruct((KEEP, targets), BF16),
            jax.ShapeDtypeStruct((KEEP, 128), jnp.int32),
            jax.ShapeDtypeStruct((8, KEEP), jnp.int32),
            jax.ShapeDtypeStruct((8, 128), F32),
        ),
        in_specs=[SMEM] + [VMEM] * 3,
        out_specs=(VMEM,) * 5,
        scratch_shapes=[pltpu.VMEM((KEEP + MOVE, packed.shape[1]), BF16)],
        compiler_params=ROOM,
        cost_estimate=pl.CostEstimate(
            flops=100_000_000, bytes_accessed=2_000_000, transcendentals=0
        ),
    )(patch_counts, packed, coming, wide)


def by_parity(values):
    part = [values[:, 128 * i : 128 * (i + 1)] for i in range(6)]
    turned = [pltpu.roll(p, 64, 1) for p in part]
    low = lax.broadcasted_iota(jnp.int32, part[0].shape, 1) < 64
    even = [part[0], jnp.where(low, part[1], turned[3]), jnp.where(low, turned[3], turned[4])]
    odd = [jnp.where(low, turned[1], turned[2]), jnp.where(low, turned[2], part[4]), part[5]]
    return jnp.concatenate(even, axis=1), jnp.concatenate(odd, axis=1)


def norm_kernel(place_ref, *refs):
    blocks, (share_ref, own_ref, other_ref, chips_ref) = refs[:-4], refs[-4:]
    me, core = place_ref[0], place_ref[1]
    width = blocks[0].shape[1]
    values = [b[...].astype(F32) for b in blocks[:-2]]
    values.append(jnp.concatenate([blocks[-2][...], blocks[-1][...]], axis=0).astype(F32))
    offsets = [0]
    for step in range(1, N_MP // 2):
        offsets += [-step, step]
    offsets.append(N_MP // 2)
    features = width * N_MP
    mean = sum(jnp.sum(v, axis=1, keepdims=True) for v in values) / features
    spread = sum(jnp.sum((v - mean) * (v - mean), axis=1, keepdims=True) for v in values)
    scale = lax.rsqrt(spread / features + 1e-06)
    half = width // 2
    for offset, v in zip(offsets, values):
        place = lax.rem(me + offset + N_MP, N_MP)
        normed = (v - mean) * scale
        chips_ref[2 * place] = normed[:, :half].astype(BF16)
        chips_ref[2 * place + 1] = normed[:, half:].astype(BF16)
        even, odd = by_parity(normed)
        first = core == 0
        columns = pl.ds(pl.multiple_of(place * half, 128), half)
        own_ref[:, columns] = jnp.where(first, even, odd).astype(BF16)
        other_ref[:, columns] = jnp.where(first, odd, even).astype(BF16)
    start = pl.multiple_of(jnp.minimum(me, SHARES - 1) * SHARE, SHARE)
    share_ref[...] = chips_ref[:, pl.ds(start, SHARE), :]


def gather_norm(own, place):
    blocks = [own]
    ahead = back = own
    for _ in range(1, N_MP // 2):
        ahead = shift(ahead, "mp", N_MP, 1)
        back = shift(back, "mp", N_MP, -1)
        blocks += [ahead, back]
    half = own.shape[0] // 2
    blocks.append(shift(ahead[:half], "mp", N_MP, 1))
    blocks.append(shift(back[half:], "mp", N_MP, -1))
    rows, width = own.shape
    return pl.pallas_call(
        norm_kernel,
        out_shape=(
            jax.ShapeDtypeStruct((2 * N_MP, SHARE, width // 2), BF16),
            jax.ShapeDtypeStruct((rows, width * N_MP // 2), BF16),
            jax.ShapeDtypeStruct((rows, width * N_MP // 2), BF16),
        ),
        in_specs=[SMEM] + [VMEM] * len(blocks),
        out_specs=(VMEM, VMEM, VMEM),
        scratch_shapes=[pltpu.VMEM((2 * N_MP, rows, width // 2), BF16)],
        compiler_params=ROOM,
        cost_estimate=pl.CostEstimate(flops=4_000_000, bytes_accessed=4_000_000, transcendentals=0),
    )(place, *blocks)


def project_kernel(own_ref, other_ref, weight_ref, own_out, other_out):
    @pl.when(pl.program_id(0) == 0)
    def _():
        own_out[...] = jnp.zeros_like(own_out)
        other_out[...] = jnp.zeros_like(other_out)

    rows = own_ref.shape[0]
    chips, groups = weight_ref.shape[:2]
    left = jnp.concatenate([own_ref[...], other_ref[...]], axis=0)
    right = jnp.concatenate(
        [
            jnp.concatenate([weight_ref[i, group] for group in range(groups)], axis=1)
            for i in range(chips)
        ],
        axis=0,
    )
    product = jnp.dot(left, right, preferred_element_type=F32)
    own_out[...] += product[:rows]
    other_out[...] += product[rows:]


def project(own, other, weight):
    rows = own.shape[0]
    chips, groups, depth, span = weight.shape
    step = 4
    block = pl.BlockSpec((rows, step * depth), lambda i: (0, i))
    result = pl.BlockSpec((rows, groups * span), lambda i: (0, 0))
    return pl.pallas_call(
        project_kernel,
        grid=(chips // step,),
        out_shape=(jax.ShapeDtypeStruct((rows, groups * span), F32),) * 2,
        in_specs=[
            block,
            block,
            pl.BlockSpec((step, groups, depth, span), lambda i: (i, 0, 0, 0)),
        ],
        out_specs=(result, result),
        compiler_params=ROOM,
        cost_estimate=pl.CostEstimate(
            flops=1_360_000_000, bytes_accessed=9_000_000, transcendentals=0
        ),
    )(own, other, weight)


def dot_t(a, b):
    return lax.dot_general(a, b, (((1,), (1,)), ((), ())), preferred_element_type=F32)


def t_dot(a, b):
    return lax.dot_general(a, b, (((0,), (0,)), ((), ())), preferred_element_type=F32)


def norm_parts(values):
    center = values - jnp.mean(values, axis=-1, keepdims=True)
    scale = lax.rsqrt(jnp.mean(center * center, axis=-1, keepdims=True) + 1e-06)
    return center * scale, scale


def norm_grad(normed, scale, cotangent):
    along = jnp.mean(cotangent * normed, axis=-1, keepdims=True)
    return scale * (cotangent - jnp.mean(cotangent, axis=-1, keepdims=True) - normed * along)


def attend_kernel(raw_ref, more_ref, row_ref, column_ref, target_ref, total_ref, grad_ref):
    inverse_root = 1.0 / math.sqrt(HD)
    heads = target_ref.shape[1] // HD
    rows = raw_ref.shape[0]
    row_segment = row_ref[:, :1]
    valid = row_segment >= 0
    allowed = (row_segment == column_ref[:1, :]) & valid
    total = total_ref[:1, :1]
    squares = jnp.zeros((raw_ref.shape[0], HD), F32)
    for head in range(heads):
        cut = [slice((part * heads + head) * HD, (part * heads + head + 1) * HD) for part in range(3)]
        query, key, value = [raw_ref[:, c] + more_ref[:, c] for c in cut]
        query_exact, query_scale = norm_parts(query)
        key_exact, key_scale = norm_parts(key)
        query_normed = query_exact.astype(BF16)
        key_normed = key_exact.astype(BF16)
        value_rows = value.astype(BF16)
        scores = dot_t(query_normed, key_normed) * inverse_root
        exponent = jnp.where(allowed, jnp.exp(scores), 0.0)
        denominator = jnp.sum(exponent, axis=-1, keepdims=True)
        denominator = jnp.where(valid, denominator, 1.0)
        weights = (exponent / denominator).astype(BF16)
        attended = jnp.dot(weights, value_rows, preferred_element_type=F32)
        target = target_ref[:, head * HD : (head + 1) * HD].astype(F32)
        error = jnp.where(valid, attended - target, 0.0)
        squares += error * error
        out_grad = (error / total).astype(BF16)
        prob_grad = dot_t(out_grad, value_rows)
        grad_ref[:rows, cut[2]] = t_dot(weights, out_grad).astype(BF16)
        weight_float = weights.astype(F32)
        inner = jnp.sum(prob_grad * weight_float, axis=-1, keepdims=True)
        score_grad = (weight_float * (prob_grad - inner) * inverse_root).astype(BF16)
        query_cotangent = jnp.dot(score_grad, key_normed, preferred_element_type=F32)
        key_cotangent = t_dot(score_grad, query_normed)
        grad_ref[:rows, cut[0]] = norm_grad(query_exact, query_scale, query_cotangent).astype(BF16)
        grad_ref[:rows, cut[1]] = norm_grad(key_exact, key_scale, key_cotangent).astype(BF16)
    square = jnp.full((STATS, grad_ref.shape[1]), jnp.sum(squares), F32)
    high = square.astype(BF16).astype(F32)
    middle = (square - high).astype(BF16).astype(F32)
    low = square - high - middle
    place = lax.broadcasted_iota(jnp.int32, square.shape, 0)
    terms = jnp.where(place == 0, high, jnp.where(place == 1, middle, low))
    grad_ref[rows:, :] = jnp.where(place < 3, terms, 0.0).astype(BF16)


def attend(raw, more, column, row, targets, patch_total):
    rows, width = raw.shape
    return pl.pallas_call(
        attend_kernel,
        out_shape=jax.ShapeDtypeStruct((rows + STATS, width), BF16),
        in_specs=[VMEM] * 6,
        out_specs=VMEM,
        compiler_params=ROOM,
        cost_estimate=pl.CostEstimate(
            flops=50_000_000, bytes_accessed=1_500_000, transcendentals=30_000
        ),
    )(raw, more, column, row, targets, patch_total)


def first_kernel(place_ref, blocks_ref, *refs):
    pieces, (own_out, other_out, own_last, other_last) = refs[:-4], refs[-4:]
    y, x, core = place_ref[0], place_ref[1], place_ref[2]
    half = blocks_ref.shape[3] // 2
    first = core == 0
    totals = [None, None]
    for index, far in enumerate((0, -1, 1, 2)):
        several = []
        for near in (0, -1, 1, 2):
            step_x = jnp.where(first, near, far)
            step_y = jnp.where(first, far, near)
            chip = lax.rem(y + step_y + SIDE, SIDE) * SIDE + lax.rem(x + step_x + SIDE, SIDE)
            several += [blocks_ref[share, chip] for share in range(SHARES)]
        wide = jnp.concatenate(several, axis=0).astype(F32).T.astype(BF16)
        own = jnp.where(first, wide[:half], wide[half:])
        other = jnp.where(first, wide[half:], wide[:half])
        if index == len(pieces):
            own_last[...] = own
            other_last[...] = other
            continue
        for side, left in enumerate((own, other)):
            product = jnp.dot(left, pieces[index][...], preferred_element_type=F32)
            totals[side] = product if totals[side] is None else totals[side] + product
    groups, _, span = own_out.shape
    for total, out_ref in zip(totals, (own_out, other_out)):
        for group in range(groups):
            out_ref[group] = total[:, group * span : (group + 1) * span]


def grad_first(place, blocks, pieces, groups):
    depth, width = pieces[0].shape
    feats = blocks.shape[3] // 2
    part = jax.ShapeDtypeStruct((groups, feats, width // groups), F32)
    last = jax.ShapeDtypeStruct((feats, depth), BF16)
    return pl.pallas_call(
        first_kernel,
        out_shape=(part, part, last, last),
        in_specs=[SMEM] + [VMEM] * (1 + len(pieces)),
        out_specs=(VMEM,) * 4,
        compiler_params=ROOM,
        cost_estimate=pl.CostEstimate(
            flops=1_000_000_000, bytes_accessed=6_000_000, transcendentals=0
        ),
    )(place, blocks, *pieces)


def last_kernel(start, left_ref, piece_ref, part_ref, out_ref):
    rows = piece_ref.shape[0]
    product = jnp.dot(
        left_ref[:, start : start + rows], piece_ref[...], preferred_element_type=F32
    )
    groups, _, span = out_ref.shape
    for group in range(groups):
        whole = part_ref[group] + product[:, group * span : (group + 1) * span]
        out_ref[group] = whole.astype(out_ref.dtype)


def grad_last(left, piece, part, dtype):
    return pl.pallas_call(
        functools.partial(last_kernel, left.shape[1] - piece.shape[0]),
        out_shape=jax.ShapeDtypeStruct(part.shape, dtype),
        in_specs=[VMEM] * 3,
        out_specs=VMEM,
        compiler_params=ROOM,
        cost_estimate=pl.CostEstimate(
            flops=170_000_000, bytes_accessed=3_000_000, transcendentals=0
        ),
    )(left, piece, part)


def finish_kernel(a_ref, b_ref, sum_ref, more_ref, total_ref, out_ref, loss_ref):
    out_ref[...] = a_ref[...] + b_ref[...].astype(F32)
    squared = sum_ref[:1, :1] + more_ref[:1, :1]
    loss_ref[...] = squared / (2.0 * total_ref[:1, :1])


def finish(a, b, squared, more, total):
    return pl.pallas_call(
        finish_kernel,
        out_shape=(jax.ShapeDtypeStruct(a.shape, F32), jax.ShapeDtypeStruct((1, 1), F32)),
        in_specs=[VMEM] * 5,
        out_specs=(VMEM, VMEM),
        compiler_params=ROOM,
        cost_estimate=pl.CostEstimate(flops=300_000, bytes_accessed=2_700_000, transcendentals=0),
    )(a, b, squared, more, total)


def near_kernel(*refs):
    blocks, (out_ref, sum_ref) = refs[:-2], refs[-2:]
    rows = blocks[0].shape[0] - STATS
    terms = 0.0
    for index, block in enumerate(blocks):
        out_ref[index * rows : (index + 1) * rows, :] = block[:rows, :]
        terms += block[rows:, :128].astype(F32)
    sum_ref[...] = jnp.broadcast_to(jnp.sum(terms, axis=0, keepdims=True), sum_ref.shape)


def near_rows(blocks):
    rows, width = blocks[0].shape
    return pl.pallas_call(
        near_kernel,
        out_shape=(
            jax.ShapeDtypeStruct((len(blocks) * (rows - STATS), width), BF16),
            jax.ShapeDtypeStruct((8, 128), F32),
        ),
        in_specs=[VMEM] * len(blocks),
        out_specs=(VMEM, VMEM),
        compiler_params=ROOM,
        cost_estimate=pl.CostEstimate(flops=100_000, bytes_accessed=1_800_000, transcendentals=0),
    )(*blocks)


def local(patches, embed_weight, project_weight, patch_counts, segment_ids, targets):
    whole_weight = lax.all_gather(project_weight.transpose(1, 0, 2), ("y", "x"), axis=0)
    y, x, core, mp = [lax.axis_index(a) for a in ("y", "x", "core", "mp")]

    packed, leaving, embed_part = pack(patches, targets, segment_ids, patch_counts, embed_weight)
    half = CHIPS * CORES // 2
    coming = lax.ppermute(leaving, DP, [(i + half, i) for i in range(half)])
    wide = lax.all_gather(embed_part, DP, axis=0, tiled=True)
    own_features, targets, column, row, total_tile = embed(patch_counts, packed, coming, wide)
    chip_blocks, own_half, other_half = gather_norm(own_features, jnp.stack([mp, core]))
    chip_share = lax.all_to_all(chip_blocks, ("y", "x"), split_axis=0, concat_axis=0, tiled=True)
    more_half, chip_share = lax.optimization_barrier((swap(other_half), chip_share))
    chip_rows = lax.all_gather(chip_share, "mp", axis=0)
    own_part, other_part = project(own_half, more_half, whole_weight)
    grad_rows = attend(own_part, swap(other_part), column, row, targets, total_tile)

    near, tile = near_rows(
        lax.optimization_barrier(
            (
                grad_rows,
                turn(grad_rows, True, 1),
                turn(grad_rows, True, -1),
                turn(grad_rows, True, 2),
            )
        )
    )
    behind, ahead = turn(near, False, 1), turn(near, False, -1)
    tile = sum((shift(tile, "mp", N_MP, step) for step in (1, 2, 3)), tile)
    tile = tile + turn(tile, False, -1)
    behind, ahead, tile = lax.optimization_barrier((behind, ahead, tile))
    opposite = turn(behind, False, 1)
    tile = tile + shift(tile, "mp", N_MP, 4)
    tile = tile + turn(tile, False, -2)
    groups = project_weight.shape[1]
    own_grad, other_grad, own_left, other_left = grad_first(
        jnp.stack([y, x, core]), chip_rows, (near, behind, ahead), groups
    )
    opposite, tile, own_grad, other_grad = lax.optimization_barrier(
        (opposite, tile, own_grad, other_grad)
    )
    more_grad, more_tile = lax.optimization_barrier(
        (swap(grad_last(other_left, opposite, other_grad, BF16)), swap(tile))
    )
    weight_grad, loss_tile = finish(
        grad_last(own_left, opposite, own_grad, F32), more_grad, tile, more_tile, total_tile
    )
    loss_value = loss_tile[0, 0]
    return (weight_grad.transpose(1, 0, 2), loss_value)


def solution(mesh):
    chips = Mesh(mesh.devices.reshape(SIDE, SIDE, CORES, N_MP), DP + ("mp",))
    in_specs = (
        P(DP, None),
        P(("mp",) + DP, None),
        P(DP, None, "mp"),
        P(DP),
        P(DP),
        P(DP, "mp"),
    )
    out_specs = (P(DP, None, "mp"), P())
    return jax.shard_map(
        local, mesh=chips, in_specs=in_specs, out_specs=out_specs, check_vma=False
    )
```

```python
import functools
import math

import jax
import jax.numpy as jnp
from jax import lax
from jax.experimental import pallas as pl
from jax.experimental.pallas import tpu as pltpu
from jax.sharding import Mesh
from jax.sharding import PartitionSpec as P

HD = 128
KEEP = 96
MOVE = 64
P_SIZE = 588
PAD_P = 640
SHARE = 16
SHARES = KEEP // SHARE
STATS = 16
SEGMENT = 600
SIDE = 4
CHIPS = 16
CORES = 2
N_MP = 8
DP = ("y", "x", "core")
F32 = jnp.float32
BF16 = jnp.bfloat16
VMEM = pl.BlockSpec(memory_space=pltpu.VMEM)
SMEM = pl.BlockSpec(memory_space=pltpu.SMEM)
ROOM = pltpu.CompilerParams(vmem_limit_bytes=48 * 1024 * 1024)


def shift(array, axis, size, step):
    return lax.ppermute(array, axis, [(i, (i + step) % size) for i in range(size)])


def swap(array):
    return lax.ppermute(array, "core", [(0, 1), (1, 0)])


def turn(array, first, step):
    pairs = []
    for y in range(SIDE):
        for x in range(SIDE):
            for core in range(CORES):
                along_x = (core == 0) == first
                to_y = y if along_x else (y + step) % SIDE
                to_x = (x + step) % SIDE if along_x else x
                pairs.append(((y * SIDE + x) * CORES + core, (to_y * SIDE + to_x) * CORES + core))
    return lax.ppermute(array, DP, pairs)


def rows_kept(counts_ref):
    end = jnp.int32(0)
    kept = jnp.int32(0)
    for slot in range(counts_ref.shape[0]):
        end = end + counts_ref[slot]
        kept = jnp.where(end <= KEEP, end, kept)
    return pl.multiple_of(kept, 16), end


def pack_kernel(counts_ref, *refs):
    sources, (all_ref, leave_ref, wide_ref, tall), rest = refs[:4], refs[4:8], refs[8:]
    places, sem = rest[:4], rest[4]
    copies = [
        pltpu.make_async_copy(source, place, sem.at[index])
        for index, (source, place) in enumerate(zip(sources, places))
    ]
    for copy in copies:
        copy.start()
    for copy in copies:
        copy.wait()
    patch_ref, target_ref, segment_ref, embed_ref = places
    p_size, rows = patch_ref.shape
    tall[...] = jnp.zeros_like(tall)
    tall[:p_size, :] = patch_ref[...].astype(F32)
    marks = jnp.broadcast_to(segment_ref[...].astype(F32) + 1.0, (8, rows))
    tall[SEGMENT : SEGMENT + 8, :] = marks
    all_ref[:rows, :PAD_P] = tall[...].T.astype(BF16)
    all_ref[:rows, PAD_P:] = target_ref[...]
    all_ref[rows:, :] = jnp.zeros((all_ref.shape[0] - rows, all_ref.shape[1]), BF16)
    kept, total = rows_kept(counts_ref)
    leave_ref[...] = all_ref[pl.ds(kept, MOVE), :]
    row = lax.broadcasted_iota(jnp.int32, (wide_ref.shape[0], wide_ref.shape[1] - 512), 0)
    column = lax.broadcasted_iota(jnp.int32, (wide_ref.shape[0], wide_ref.shape[1] - 512), 1)
    here = (row == 0) & (column == p_size - 512)
    wide_ref[:, 512:] = jnp.where(here, total.astype(F32), 0.0).astype(BF16)
    wide_ref[:, :p_size] = embed_ref[...]


def pack(patches, targets, segment_ids, patch_counts, embed_weight):
    rows, p_size = patches.shape
    width = PAD_P + targets.shape[1]
    return pl.pallas_call(
        pack_kernel,
        out_shape=(
            jax.ShapeDtypeStruct((rows + MOVE, width), BF16),
            jax.ShapeDtypeStruct((MOVE, width), BF16),
            jax.ShapeDtypeStruct((embed_weight.shape[0], PAD_P), BF16),
        ),
        in_specs=[SMEM] + [pl.BlockSpec(memory_space=pltpu.HBM)] * 4,
        out_specs=(VMEM, VMEM, VMEM),
        scratch_shapes=[
            pltpu.VMEM((PAD_P, rows), F32),
            pltpu.VMEM((p_size, rows), BF16),
            pltpu.VMEM(targets.shape, BF16),
            pltpu.VMEM((1, rows), jnp.int32),
            pltpu.VMEM(embed_weight.shape, BF16),
            pltpu.SemaphoreType.DMA((4,)),
        ],
        cost_estimate=pl.CostEstimate(flops=1_000_000, bytes_accessed=1_000_000, transcendentals=0),
    )(patch_counts, patches.T, targets, segment_ids.reshape(1, rows), embed_weight)


def embed_kernel(counts_ref, all_ref, come_ref, wide_ref, out_ref, target_ref, column_ref, row_ref, total_ref, around):
    kept, _ = rows_kept(counts_ref)
    around[...] = jnp.zeros_like(around)
    around[pl.ds(kept, MOVE), :] = come_ref[...]
    mine = lax.broadcasted_iota(jnp.int32, (KEEP, 1), 0) < kept
    merged = jnp.where(mine, all_ref[:KEEP, :], around[:KEEP, :])
    target_ref[...] = merged[:, PAD_P:]
    marks = merged[:, PAD_P - 128 : PAD_P].astype(F32)
    slot = lax.broadcasted_iota(jnp.int32, marks.shape, 1) == SEGMENT - (PAD_P - 128)
    mark = jnp.sum(jnp.where(slot, marks, 0.0), axis=1, keepdims=True) - 1.0
    spread = jnp.broadcast_to(mark, marks.shape)
    column_ref[...] = spread.astype(jnp.int32)
    row_ref[...] = spread.T[:8, :].astype(jnp.int32)
    tail = wide_ref[:, PAD_P - 128 : PAD_P].astype(F32)
    slot = lax.broadcasted_iota(jnp.int32, tail.shape, 1) == P_SIZE - (PAD_P - 128)
    total_ref[...] = jnp.full(total_ref.shape, jnp.sum(jnp.where(slot, tail, 0.0)), F32)
    out_ref[...] = dot_t(merged[:, :PAD_P], wide_ref[...]).astype(BF16)


def embed(patch_counts, packed, coming, wide):
    targets = packed.shape[1] - PAD_P
    return pl.pallas_call(
        embed_kernel,
        out_shape=(
            jax.ShapeDtypeStruct((KEEP, wide.shape[0]), BF16),
            jax.ShapeDtypeStruct((KEEP, targets), BF16),
            jax.ShapeDtypeStruct((KEEP, 128), jnp.int32),
            jax.ShapeDtypeStruct((8, KEEP), jnp.int32),
            jax.ShapeDtypeStruct((8, 128), F32),
        ),
        in_specs=[SMEM] + [VMEM] * 3,
        out_specs=(VMEM,) * 5,
        scratch_shapes=[pltpu.VMEM((KEEP + MOVE, packed.shape[1]), BF16)],
        compiler_params=ROOM,
        cost_estimate=pl.CostEstimate(
            flops=100_000_000, bytes_accessed=2_000_000, transcendentals=0
        ),
    )(patch_counts, packed, coming, wide)


def by_parity(values):
    part = [values[:, 128 * i : 128 * (i + 1)] for i in range(6)]
    turned = [pltpu.roll(p, 64, 1) for p in part]
    low = lax.broadcasted_iota(jnp.int32, part[0].shape, 1) < 64
    even = [part[0], jnp.where(low, part[1], turned[3]), jnp.where(low, turned[3], turned[4])]
    odd = [jnp.where(low, turned[1], turned[2]), jnp.where(low, turned[2], part[4]), part[5]]
    return jnp.concatenate(even, axis=1), jnp.concatenate(odd, axis=1)


def norm_kernel(place_ref, *refs):
    blocks, (share_ref, own_ref, other_ref, chips_ref) = refs[:-4], refs[-4:]
    me, core = place_ref[0], place_ref[1]
    width = blocks[0].shape[1]
    values = [b[...].astype(F32) for b in blocks[:-2]]
    values.append(jnp.concatenate([blocks[-2][...], blocks[-1][...]], axis=0).astype(F32))
    offsets = [0]
    for step in range(1, N_MP // 2):
        offsets += [-step, step]
    offsets.append(N_MP // 2)
    features = width * N_MP
    mean = sum(jnp.sum(v, axis=1, keepdims=True) for v in values) / features
    spread = sum(jnp.sum((v - mean) * (v - mean), axis=1, keepdims=True) for v in values)
    scale = lax.rsqrt(spread / features + 1e-06)
    half = width // 2
    for offset, v in zip(offsets, values):
        place = lax.rem(me + offset + N_MP, N_MP)
        normed = (v - mean) * scale
        chips_ref[2 * place] = normed[:, :half].astype(BF16)
        chips_ref[2 * place + 1] = normed[:, half:].astype(BF16)
        even, odd = by_parity(normed)
        first = core == 0
        columns = pl.ds(pl.multiple_of(place * half, 128), half)
        own_ref[:, columns] = jnp.where(first, even, odd).astype(BF16)
        other_ref[:, columns] = jnp.where(first, odd, even).astype(BF16)
    start = pl.multiple_of(jnp.minimum(me, SHARES - 1) * SHARE, SHARE)
    share_ref[...] = chips_ref[:, pl.ds(start, SHARE), :]


def gather_norm(own, place):
    half = own.shape[0] // 2
    one, two = [(shift(own, "mp", N_MP, k), shift(own, "mp", N_MP, -k)) for k in (1, 2)]
    one, two = lax.optimization_barrier((one, two))
    three = (shift(two[0], "mp", N_MP, 1), shift(two[1], "mp", N_MP, -1))
    four = (shift(two[0][:half], "mp", N_MP, 2), shift(two[1][half:], "mp", N_MP, -2))
    blocks = [own, *one, *two, *three, *four]
    rows, width = own.shape
    return pl.pallas_call(
        norm_kernel,
        out_shape=(
            jax.ShapeDtypeStruct((2 * N_MP, SHARE, width // 2), BF16),
            jax.ShapeDtypeStruct((rows, width * N_MP // 2), BF16),
            jax.ShapeDtypeStruct((rows, width * N_MP // 2), BF16),
        ),
        in_specs=[SMEM] + [VMEM] * len(blocks),
        out_specs=(VMEM, VMEM, VMEM),
        scratch_shapes=[pltpu.VMEM((2 * N_MP, rows, width // 2), BF16)],
        compiler_params=ROOM,
        cost_estimate=pl.CostEstimate(flops=4_000_000, bytes_accessed=4_000_000, transcendentals=0),
    )(place, *blocks)


def project_kernel(own_ref, other_ref, weight_ref, own_out, other_out):
    @pl.when(pl.program_id(0) == 0)
    def _():
        own_out[...] = jnp.zeros_like(own_out)
        other_out[...] = jnp.zeros_like(other_out)

    rows = own_ref.shape[0]
    chips, groups = weight_ref.shape[:2]
    left = jnp.concatenate([own_ref[...], other_ref[...]], axis=0)
    right = jnp.concatenate(
        [
            jnp.concatenate([weight_ref[i, group] for group in range(groups)], axis=1)
            for i in range(chips)
        ],
        axis=0,
    )
    product = jnp.dot(left, right, preferred_element_type=F32)
    own_out[...] += product[:rows]
    other_out[...] += product[rows:]


def project(own, other, weight):
    rows = own.shape[0]
    chips, groups, depth, span = weight.shape
    step = 4
    block = pl.BlockSpec((rows, step * depth), lambda i: (0, i))
    result = pl.BlockSpec((rows, groups * span), lambda i: (0, 0))
    return pl.pallas_call(
        project_kernel,
        grid=(chips // step,),
        out_shape=(jax.ShapeDtypeStruct((rows, groups * span), F32),) * 2,
        in_specs=[
            block,
            block,
            pl.BlockSpec((step, groups, depth, span), lambda i: (i, 0, 0, 0)),
        ],
        out_specs=(result, result),
        compiler_params=ROOM,
        cost_estimate=pl.CostEstimate(
            flops=1_360_000_000, bytes_accessed=9_000_000, transcendentals=0
        ),
    )(own, other, weight)


def dot_t(a, b):
    return lax.dot_general(a, b, (((1,), (1,)), ((), ())), preferred_element_type=F32)


def t_dot(a, b):
    return lax.dot_general(a, b, (((0,), (0,)), ((), ())), preferred_element_type=F32)


def norm_parts(values):
    center = values - jnp.mean(values, axis=-1, keepdims=True)
    scale = lax.rsqrt(jnp.mean(center * center, axis=-1, keepdims=True) + 1e-06)
    return center * scale, scale


def norm_grad(normed, scale, cotangent):
    along = jnp.mean(cotangent * normed, axis=-1, keepdims=True)
    return scale * (cotangent - jnp.mean(cotangent, axis=-1, keepdims=True) - normed * along)


def attend_kernel(raw_ref, more_ref, row_ref, column_ref, target_ref, total_ref, grad_ref):
    inverse_root = 1.0 / math.sqrt(HD)
    heads = target_ref.shape[1] // HD
    rows = raw_ref.shape[0]
    row_segment = row_ref[:, :1]
    valid = row_segment >= 0
    allowed = (row_segment == column_ref[:1, :]) & valid
    total = total_ref[:1, :1]
    squares = jnp.zeros((raw_ref.shape[0], HD), F32)
    for head in range(heads):
        cut = [slice((part * heads + head) * HD, (part * heads + head + 1) * HD) for part in range(3)]
        query, key, value = [raw_ref[:, c] + more_ref[:, c] for c in cut]
        query_exact, query_scale = norm_parts(query)
        key_exact, key_scale = norm_parts(key)
        query_normed = query_exact.astype(BF16)
        key_normed = key_exact.astype(BF16)
        value_rows = value.astype(BF16)
        scores = dot_t(query_normed, key_normed) * inverse_root
        exponent = jnp.where(allowed, jnp.exp(scores), 0.0)
        denominator = jnp.sum(exponent, axis=-1, keepdims=True)
        denominator = jnp.where(valid, denominator, 1.0)
        weights = (exponent / denominator).astype(BF16)
        attended = jnp.dot(weights, value_rows, preferred_element_type=F32)
        target = target_ref[:, head * HD : (head + 1) * HD].astype(F32)
        error = jnp.where(valid, attended - target, 0.0)
        squares += error * error
        out_grad = (error / total).astype(BF16)
        prob_grad = dot_t(out_grad, value_rows)
        grad_ref[:rows, cut[2]] = t_dot(weights, out_grad).astype(BF16)
        weight_float = weights.astype(F32)
        inner = jnp.sum(prob_grad * weight_float, axis=-1, keepdims=True)
        score_grad = (weight_float * (prob_grad - inner) * inverse_root).astype(BF16)
        query_cotangent = jnp.dot(score_grad, key_normed, preferred_element_type=F32)
        key_cotangent = t_dot(score_grad, query_normed)
        grad_ref[:rows, cut[0]] = norm_grad(query_exact, query_scale, query_cotangent).astype(BF16)
        grad_ref[:rows, cut[1]] = norm_grad(key_exact, key_scale, key_cotangent).astype(BF16)
    square = jnp.full((STATS, grad_ref.shape[1]), jnp.sum(squares), F32)
    high = square.astype(BF16).astype(F32)
    middle = (square - high).astype(BF16).astype(F32)
    low = square - high - middle
    place = lax.broadcasted_iota(jnp.int32, square.shape, 0)
    terms = jnp.where(place == 0, high, jnp.where(place == 1, middle, low))
    grad_ref[rows:, :] = jnp.where(place < 3, terms, 0.0).astype(BF16)


def attend(raw, more, column, row, targets, patch_total):
    rows, width = raw.shape
    return pl.pallas_call(
        attend_kernel,
        out_shape=jax.ShapeDtypeStruct((rows + STATS, width), BF16),
        in_specs=[VMEM] * 6,
        out_specs=VMEM,
        compiler_params=ROOM,
        cost_estimate=pl.CostEstimate(
            flops=50_000_000, bytes_accessed=1_500_000, transcendentals=30_000
        ),
    )(raw, more, column, row, targets, patch_total)


def first_kernel(place_ref, blocks_ref, *refs):
    pieces, (own_out, other_out, own_last, other_last) = refs[:-4], refs[-4:]
    y, x, core = place_ref[0], place_ref[1], place_ref[2]
    half = blocks_ref.shape[3] // 2
    first = core == 0
    totals = [None, None]
    for index, far in enumerate((0, -1, 1, 2)):
        several = []
        for near in (0, -1, 1, 2):
            step_x = jnp.where(first, near, far)
            step_y = jnp.where(first, far, near)
            chip = lax.rem(y + step_y + SIDE, SIDE) * SIDE + lax.rem(x + step_x + SIDE, SIDE)
            several += [blocks_ref[share, chip] for share in range(SHARES)]
        wide = jnp.concatenate(several, axis=0).astype(F32).T.astype(BF16)
        own = jnp.where(first, wide[:half], wide[half:])
        other = jnp.where(first, wide[half:], wide[:half])
        if index == len(pieces):
            own_last[...] = own
            other_last[...] = other
            continue
        for side, left in enumerate((own, other)):
            product = jnp.dot(left, pieces[index][...], preferred_element_type=F32)
            totals[side] = product if totals[side] is None else totals[side] + product
    groups, _, span = own_out.shape
    for total, out_ref in zip(totals, (own_out, other_out)):
        for group in range(groups):
            out_ref[group] = total[:, group * span : (group + 1) * span]


def grad_first(place, blocks, pieces, groups):
    depth, width = pieces[0].shape
    feats = blocks.shape[3] // 2
    part = jax.ShapeDtypeStruct((groups, feats, width // groups), F32)
    last = jax.ShapeDtypeStruct((feats, depth), BF16)
    return pl.pallas_call(
        first_kernel,
        out_shape=(part, part, last, last),
        in_specs=[SMEM] + [VMEM] * (1 + len(pieces)),
        out_specs=(VMEM,) * 4,
        compiler_params=ROOM,
        cost_estimate=pl.CostEstimate(
            flops=1_000_000_000, bytes_accessed=6_000_000, transcendentals=0
        ),
    )(place, blocks, *pieces)


def last_kernel(start, left_ref, piece_ref, part_ref, out_ref):
    rows = piece_ref.shape[0]
    product = jnp.dot(
        left_ref[:, start : start + rows], piece_ref[...], preferred_element_type=F32
    )
    groups, _, span = out_ref.shape
    for group in range(groups):
        whole = part_ref[group] + product[:, group * span : (group + 1) * span]
        out_ref[group] = whole.astype(out_ref.dtype)


def grad_last(left, piece, part, dtype):
    return pl.pallas_call(
        functools.partial(last_kernel, left.shape[1] - piece.shape[0]),
        out_shape=jax.ShapeDtypeStruct(part.shape, dtype),
        in_specs=[VMEM] * 3,
        out_specs=VMEM,
        compiler_params=ROOM,
        cost_estimate=pl.CostEstimate(
            flops=170_000_000, bytes_accessed=3_000_000, transcendentals=0
        ),
    )(left, piece, part)


def finish_kernel(a_ref, b_ref, sum_ref, more_ref, total_ref, out_ref, loss_ref):
    out_ref[...] = a_ref[...] + b_ref[...].astype(F32)
    squared = sum_ref[:1, :1] + more_ref[:1, :1]
    loss_ref[...] = squared / (2.0 * total_ref[:1, :1])


def finish(a, b, squared, more, total):
    return pl.pallas_call(
        finish_kernel,
        out_shape=(jax.ShapeDtypeStruct(a.shape, F32), jax.ShapeDtypeStruct((1, 1), F32)),
        in_specs=[VMEM] * 5,
        out_specs=(VMEM, VMEM),
        compiler_params=ROOM,
        cost_estimate=pl.CostEstimate(flops=300_000, bytes_accessed=2_700_000, transcendentals=0),
    )(a, b, squared, more, total)


def near_kernel(*refs):
    blocks, (out_ref, sum_ref) = refs[:-2], refs[-2:]
    rows = blocks[0].shape[0] - STATS
    terms = 0.0
    for index, block in enumerate(blocks):
        out_ref[index * rows : (index + 1) * rows, :] = block[:rows, :]
        terms += block[rows:, :128].astype(F32)
    sum_ref[...] = jnp.broadcast_to(jnp.sum(terms, axis=0, keepdims=True), sum_ref.shape)


def near_rows(blocks):
    rows, width = blocks[0].shape
    return pl.pallas_call(
        near_kernel,
        out_shape=(
            jax.ShapeDtypeStruct((len(blocks) * (rows - STATS), width), BF16),
            jax.ShapeDtypeStruct((8, 128), F32),
        ),
        in_specs=[VMEM] * len(blocks),
        out_specs=(VMEM, VMEM),
        compiler_params=ROOM,
        cost_estimate=pl.CostEstimate(flops=100_000, bytes_accessed=1_800_000, transcendentals=0),
    )(*blocks)


def local(patches, embed_weight, project_weight, patch_counts, segment_ids, targets):
    whole_weight = lax.all_gather(project_weight.transpose(1, 0, 2), ("y", "x"), axis=0)
    y, x, core, mp = [lax.axis_index(a) for a in ("y", "x", "core", "mp")]

    packed, leaving, embed_part = pack(patches, targets, segment_ids, patch_counts, embed_weight)
    half = CHIPS * CORES // 2
    coming = lax.ppermute(leaving, DP, [(i + half, i) for i in range(half)])
    wide = lax.all_gather(embed_part, DP, axis=0, tiled=True)
    own_features, targets, column, row, total_tile = embed(patch_counts, packed, coming, wide)
    chip_blocks, own_half, other_half = gather_norm(own_features, jnp.stack([mp, core]))
    chip_share = lax.all_to_all(chip_blocks, ("y", "x"), split_axis=0, concat_axis=0, tiled=True)
    more_half, chip_share = lax.optimization_barrier((swap(other_half), chip_share))
    chip_rows = lax.all_gather(chip_share, "mp", axis=0)
    own_part, other_part = project(own_half, more_half, whole_weight)
    grad_rows = attend(own_part, swap(other_part), column, row, targets, total_tile)

    near, tile = near_rows(
        lax.optimization_barrier(
            (
                grad_rows,
                turn(grad_rows, True, 1),
                turn(grad_rows, True, -1),
                turn(grad_rows, True, 2),
            )
        )
    )
    behind, ahead = turn(near, False, 1), turn(near, False, -1)
    tile = sum((shift(tile, "mp", N_MP, step) for step in (1, 2, 3)), tile)
    tile = tile + turn(tile, False, -1)
    behind, ahead, tile = lax.optimization_barrier((behind, ahead, tile))
    opposite = turn(behind, False, 1)
    tile = tile + shift(tile, "mp", N_MP, 4)
    tile = tile + turn(tile, False, -2)
    groups = project_weight.shape[1]
    own_grad, other_grad, own_left, other_left = grad_first(
        jnp.stack([y, x, core]), chip_rows, (near, behind, ahead), groups
    )
    opposite, tile, own_grad, other_grad = lax.optimization_barrier(
        (opposite, tile, own_grad, other_grad)
    )
    more_grad, more_tile = lax.optimization_barrier(
        (swap(grad_last(other_left, opposite, other_grad, BF16)), swap(tile))
    )
    weight_grad, loss_tile = finish(
        grad_last(own_left, opposite, own_grad, F32), more_grad, tile, more_tile, total_tile
    )
    loss_value = loss_tile[0, 0]
    return (weight_grad.transpose(1, 0, 2), loss_value)


def solution(mesh):
    chips = Mesh(mesh.devices.reshape(SIDE, SIDE, CORES, N_MP), DP + ("mp",))
    in_specs = (
        P(DP, None),
        P(("mp",) + DP, None),
        P(DP, None, "mp"),
        P(DP),
        P(DP),
        P(DP, "mp"),
    )
    out_specs = (P(DP, None, "mp"), P())
    return jax.shard_map(
        local, mesh=chips, in_specs=in_specs, out_specs=out_specs, check_vma=False
    )
```
